32 devices in a mesh: runs: 2 (over x), gx: 16 (over z, y, core).
Axes of the slice: x: 2, y: 2, z: 4, core: 2. Of those that a mesh axis runs over, the one named last changes fastest.
Arguments:
- initial: float32 [8, 512, 2048], P('runs', 'gx'), parts along dimension 0, may hold values from -3 to 3
- kappa: float32 [8, 512, 2048], P('runs', 'gx'), parts along dimension 0, may hold values from 0.3 to 1.3
- rate: float32 [8, 512, 2048], P('runs', 'gx'), parts along dimension 0, may hold values from 0.1 to 1
- writer: int32 [4, 2048, 1], P('runs', 'gx'), parts along dimension 0, may hold values from 0 to 15; in each aligned block of 128 rows (0 to 127, 128 to 255, ..., all dimensions but the last counted through in order) at most 16 rows name the same one
Outputs:
- final_state: float32 [8, 512, 2048], P('runs', 'gx'), parts along dimension 0
- snapshots: bfloat16 [4, 4096, 2048], P('runs', 'gx'), parts along dimension 0
The draws below stay inside these ranges and needn't reach their ends.
There are 2 independent parts, one for each index of `runs`. The reference program is written for one: setup_inputs(seed, part) draws one part's arguments, and reference() takes and returns one part's arrays. A program takes and returns all parts, laid end to end along the dimension named above; each array names one. Nothing has to cross between parts.
Inputs may be any that keep to these rules, and one draw needn't show every extreme that they name: `writer`: in each aligned block of 128 rows (one device's rows of one step) no destination is named more than 16 times, and one is named exactly 16 times.
All inputs are finite; a program needn't handle non-finite values.
Results may differ from the reference program's by a relative error of at most 0.001.
Values may be sent and summed in bfloat16 or wider, within the bound.
No kernel may reach another device: no remote copies, remote signals or barrier semaphores. Data moves between devices by JAX's collectives and lax.ppermute only.
A program may use at most 64 MiB of HBM per device.

```python
import math
import jax
import jax.numpy as jnp
import numpy as np

CX = 32
NY = 2048
LEV = 4
STEPS = 2
NX = 512
SLABS = 2048
CAP = 16
N_GX = 16


def shard_levels(stream_key, shape, pieces, low, largest):
    factor_of, own = 1.0, jax.random.fold_in(stream_key, 6)
    for dim, shards_of in pieces:
        steps = jnp.exp(jax.random.uniform(jax.random.fold_in(own, dim), (shards_of,), jnp.float32, low / len(pieces), largest / len(pieces)))
        factor_of = factor_of * jnp.repeat(steps, shape[dim] // shards_of).reshape([-1 if axis == dim else 1 for axis in range(len(shape))])
    return factor_of


def deal_out(rng, own, number, rows, count, top, bound, lean):
    ranking = jax.random.permutation(rng, count)
    packed, usual = portions_of(count, rows * top, bound, lean, True), portions_of(count, rows * top, bound, lean, False)
    places = jnp.arange(count)

    def named(tallies, rotation):
        used = int((tallies > 0).sum())
        fixed = max(1, used // 4)
        moved = fixed + (places - fixed + rotation * (used - fixed)) % max(1, count - fixed)
        return jnp.zeros((count,), jnp.int32).at[ranking[jnp.where(places < fixed, places, moved)]].set(jnp.asarray(tallies, jnp.int32))

    tallies = jnp.where(number % 4 == 0, named(packed, number // 4), named(usual, number - number // 4 - 1))
    mixed = jax.random.permutation(jax.random.fold_in(own, 3), count)
    donor, taker = mixed[0:count // 2 * 2:2], mixed[1:count // 2 * 2:2]
    margin = jnp.minimum(tallies[donor] - 1, bound - tallies[taker]) // 2
    margin = jnp.where((donor == ranking[0]) | (taker == ranking[0]) | (tallies[taker] == 0), 0, jnp.maximum(margin, 0))
    moved = jax.random.randint(jax.random.fold_in(own, 4), (count // 2,), 0, 1 << 20) % (margin + 1)
    tallies = tallies.at[donor].add(-moved).at[taker].add(moved)
    labels = jnp.searchsorted(jnp.cumsum(tallies), jnp.arange(rows * top), side="right").astype(jnp.int32)
    listing = labels.reshape(top, rows).T
    listing = listing[jax.random.permutation(jax.random.fold_in(own, 1), rows)]
    rotation = jax.random.randint(jax.random.fold_in(own, 2), (rows, 1), 0, top)
    return jnp.take_along_axis(listing, (jnp.arange(top)[None, :] + rotation) % top, axis=1)


def portions_of(amount, total, most, skew, full):
    weights = [(1 << 20) // math.isqrt(rank ** skew) + 1 for rank in range(1, amount + 1)]
    largest = most if full else min(most, max(-(-total // amount), total * weights[0] // sum(weights)))
    least = 1 if total - largest >= amount - 1 else 0
    given, rest = [largest] + [least] * (amount - 1), total - largest - least * (amount - 1)
    while rest > 0:
        candidates = [i for i in range(1, amount) if given[i] < largest] or [i for i in range(1, amount) if given[i] < most]
        whole, remaining = sum([weights[i] for i in candidates]), rest
        for i in candidates:
            more = min(most - given[i], max(1, remaining * weights[i] // whole), rest)
            given[i] = given[i] + more
            rest = rest - more
    return np.array(given)


def centred(rng, extent, scale, reach, shards=(), held_as=jnp.bfloat16):
    entries = scale * jax.random.normal(rng, extent, jnp.float32)
    if shards:
        entries = entries * shard_levels(rng, extent, shards, -0.22, 0.18)
    return jnp.clip(entries, -reach, reach).astype(held_as)


def setup_inputs(seed: int = 0, part: int = 0) -> dict:
    splits = jax.random.split(jax.random.key(seed), 5)
    part_keys = jax.random.split(jax.random.fold_in(splits[4], part), 5)
    initial = centred(part_keys[0], (LEV, NX, NY), 1.0, 3.0, ((1, 16),), jnp.float32)
    kappa = jnp.clip(0.3 + 0.99999994 * jax.random.uniform(part_keys[1], (LEV, NX, NY), jnp.float32) ** shard_levels(part_keys[1], (LEV, NX, NY), ((1, 16),), -0.2, 0.2), 0.3, 1.3)
    rate = jnp.clip(jnp.exp(math.log(1.0) - 2.3025851 * jax.random.uniform(part_keys[2], (LEV, NX, NY), jnp.float32) ** shard_levels(part_keys[2], (LEV, NX, NY), ((1, 16),), -0.2, 0.2)), 0.1, 1.0)
    writer_keys = jax.random.split(jax.random.fold_in(part_keys[3], 1), STEPS * SLABS // (CX * LEV))
    writer_turns = jax.random.permutation(jax.random.fold_in(part_keys[3], 3), STEPS * SLABS // (CX * LEV))
    writer = jax.vmap(lambda own, number: deal_out(jax.random.fold_in(part_keys[3], 2), own, number, CX * LEV, N_GX, 1, CAP, 2))(writer_keys, writer_turns).reshape((STEPS, SLABS, 1))
    return dict(initial=initial, kappa=kappa, rate=rate, writer=writer)


DT = 0.15


def tendency(field, conduct, growth):
    centre = field[:, 1:-1]
    cond_mid = conduct[:, 1:-1]
    cond_left = 0.5 * (conduct[:, :-2] + cond_mid)
    cond_right = 0.5 * (conduct[:, 2:] + cond_mid)
    laplace = cond_left * (field[:, :-2] - centre) + cond_right * (field[:, 2:] - centre)
    cond_y = 0.5 * (cond_mid + jnp.roll(cond_mid, -1, 2))
    flux_y = cond_y * (jnp.roll(centre, -1, 2) - centre)
    laplace = laplace + flux_y - jnp.roll(flux_y, 1, 2)
    flux_z = 0.5 * (cond_mid[1:] + cond_mid[:-1]) * (centre[1:] - centre[:-1])
    zero_row = jnp.zeros_like(flux_z[:1])
    laplace = laplace + jnp.concatenate([flux_z, zero_row], 0) - jnp.concatenate([zero_row, flux_z], 0)
    return laplace + growth * centre * (1.0 - centre)


def pad_rows(field):
    return jnp.pad(field, ((0, 0), (1, 1), (0, 0)))


def route(snap_rows, dest):
    per_dev = CX * LEV
    grouped = dest.reshape(N_GX, per_dev)
    onehot = (grouped[:, :, None] == jnp.arange(N_GX, dtype=jnp.int32)[None, None, :]).astype(jnp.int32)
    before = jnp.cumsum(onehot, axis=1) - onehot
    ranks = jnp.sum(before * onehot, axis=2).astype(jnp.int32)
    targets = grouped * (N_GX * CAP) + jnp.arange(N_GX, dtype=jnp.int32)[:, None] * CAP + ranks
    result = jnp.zeros((N_GX * N_GX * CAP, NY), jnp.bfloat16)
    return result.at[targets.reshape(-1).astype(jnp.int32)].set(snap_rows)


def reference(initial, kappa, rate, writer):
    cond_pad = pad_rows(kappa)
    state = initial
    frames = []
    for step_index in range(STEPS):
        section_one = state + DT * tendency(pad_rows(state), cond_pad, rate)
        section_two = 0.75 * state + 0.25 * (section_one + DT * tendency(pad_rows(section_one), cond_pad, rate))
        state = state / 3.0 + (2.0 / 3.0) * (section_two + DT * tendency(pad_rows(section_two), cond_pad, rate))
        snap_rows = state.astype(jnp.bfloat16).reshape(LEV, N_GX, CX, NY).transpose(1, 0, 2, 3).reshape(N_GX * LEV * CX, NY)
        frames.append(route(snap_rows, writer[step_index, :, 0]))
    return state, jnp.stack(frames)
```

```python
import functools

import jax
import jax.numpy as jnp
from jax import lax
from jax.experimental import pallas as pl
from jax.experimental.pallas import tpu as pltpu
from jax.sharding import PartitionSpec as P

STEPS = 2
DT = 0.15
LANES = 128
TILE = 8
VMEM = 48 * 1024 * 1024


def step_kernel(second, *refs):
    if second:
        where_ref, u_ref, k_ref, r_ref, core_ref, chip_ref, core2_ref, chip2_ref, place_ref = refs[:9]
        refs = refs[9:]
    else:
        where_ref, u_ref, k_ref, r_ref, core_ref, chip_ref, place_ref = refs[:7]
        core2_ref = chip2_ref = None
        refs = refs[7:]
    new_ref, pack_ref, face_ref = (refs[0], refs[1], None) if second else refs[:3]
    u0, u1, u2, xp, xm, yp, ym, zp, lin, quad = refs[-10:]
    levels, rows, cells = u_ref.shape
    ext = rows + TILE
    chunks = cells // LANES
    even = where_ref[0] == 0
    row8 = lax.broadcasted_iota(jnp.int32, (TILE, LANES), 0)
    lane = lax.broadcasted_iota(jnp.int32, (ext, LANES), 1)
    low = row8 < TILE // 2
    live = jnp.where(low, where_ref[1], where_ref[2]) > 0

    def cols(j):
        j = j % chunks
        return slice(j * LANES, (j + 1) * LANES)

    def pick(core, chip):
        below = jnp.where(even, core, chip)
        above = jnp.where(even, chip, core)
        return below, above

    kk = u2
    for j in range(chunks):
        c = cols(j)
        core, chip = core_ref[:, c].astype(jnp.float32), chip_ref[:, c].astype(jnp.float32)
        if second:
            core2, chip2 = core2_ref[:, c].astype(jnp.float32), chip2_ref[:, c].astype(jnp.float32)
        for l in range(levels):
            t = slice(l * TILE, (l + 1) * TILE)
            below, above = pick(core[t], chip[t])
            k_face = jnp.where(low, pltpu.roll(below, 3, 0), pltpu.roll(above, 5, 0))
            r_face = jnp.where(low, pltpu.roll(below, 5, 0), pltpu.roll(above, 3, 0))
            if second:
                h = slice(l // 2 * TILE, (l // 2 + 1) * TILE)
                below, above = pick(core2[h], chip2[h])
                if l % 2:
                    u_face = jnp.where(low, pltpu.roll(below, 4, 0), above)
                else:
                    u_face = jnp.where(low, below, pltpu.roll(above, 4, 0))
            else:
                u_face = jnp.where(low, below, above)
            kk[l, :rows, c] = k_ref[l, :, c]
            kk[l, rows:, c] = k_face
            u0[l, :rows, c] = u_ref[l, :, c]
            u0[l, rows:, c] = u_face
            quad[l, :rows, c] = DT * r_ref[l, :, c]
            quad[l, rows:, c] = DT * r_face

    def left_right(src, l):
        right, left, here = {}, {}, {}

        def rots(j):
            j = j % chunks
            if j not in here:
                v = src[l, :, cols(j)]
                here[j] = v
                right[j] = pltpu.roll(v, LANES - 1, 1)
                left[j] = pltpu.roll(v, 1, 1)
            return j

        def at(j):
            a, b, d = rots(j - 1), rots(j), rots(j + 1)
            return (
                here[b],
                jnp.where(lane == LANES - 1, right[d], right[b]),
                jnp.where(lane == 0, left[a], left[b]),
            )

        return at

    half = 0.5 * DT
    ats = [left_right(kk, l) for l in range(levels)]
    for j in range(chunks):
        c = cols(j)
        for l in range(levels):
            k, k_right, k_left = ats[l](j)
            a = half * (k + pltpu.roll(k, ext - 1, 0))
            b = pltpu.roll(a, 1, 0)
            d, e = half * (k + k_right), half * (k + k_left)
            xp[l, :, c], xm[l, :, c], yp[l, :, c], ym[l, :, c] = a, b, d, e
            total = a + b + d + e
            if l < levels - 1:
                f = half * (k + kk[l + 1, :, c])
                zp[l, :, c] = f
                total = total + f
            if l > 0:
                total = total + zp[l - 1, :, c]
            lin[l, :, c] = 1.0 + quad[l, :, c] - total

    def euler(src, ats, l, j):
        c = cols(j)
        u, u_right, u_left = ats[l](j)
        out = u * (lin[l, :, c] - quad[l, :, c] * u)
        out = out + xp[l, :, c] * pltpu.roll(u, ext - 1, 0) + xm[l, :, c] * pltpu.roll(u, 1, 0)
        out = out + yp[l, :, c] * u_right + ym[l, :, c] * u_left
        if l < levels - 1:
            out = out + zp[l, :, c] * src[l + 1, :, c]
        if l > 0:
            out = out + zp[l - 1, :, c] * src[l - 1, :, c]
        return out

    def masked(dst, l, c, v):
        dst[l, :rows, c] = v[:rows]
        dst[l, rows:, c] = jnp.where(live, v[rows:], 0.0)

    ats = [left_right(u0, l) for l in range(levels)]
    for j in range(chunks):
        for l in range(levels):
            masked(u1, l, cols(j), euler(u0, ats, l, j))
    ats = [left_right(u1, l) for l in range(levels)]
    for j in range(chunks):
        for l in range(levels):
            c = cols(j)
            masked(u2, l, c, 0.75 * u0[l, :, c] + 0.25 * euler(u1, ats, l, j))
    ats = [left_right(u2, l) for l in range(levels)]
    for j in range(chunks):
        for l in range(levels):
            c = cols(j)
            v = (1.0 / 3.0) * u0[l, :, c] + (2.0 / 3.0) * euler(u2, ats, l, j)
            new_ref[l, :, c] = v[:rows]
    if face_ref is not None:
        half8 = row8 < TILE // 2
        for j in range(chunks):
            c = cols(j)
            for side in range(2):
                parts = []
                for h in range(levels // 2):
                    if side == 0:
                        x = new_ref[2 * h, :TILE, c]
                        y = pltpu.roll(new_ref[2 * h + 1, :TILE, c], 4, 0)
                    else:
                        x = pltpu.roll(new_ref[2 * h, rows - TILE :, c], 4, 0)
                        y = new_ref[2 * h + 1, rows - TILE :, c]
                    parts.append(jnp.where(half8, x, y))
                face_ref[side, :, c] = jnp.concatenate(parts, 0).astype(jnp.bfloat16)
    wide = 2 * LANES
    place = place_ref[...]
    for j in range(0, cells, wide):
        v = new_ref[:, :, j : j + wide].astype(jnp.bfloat16).reshape(levels * rows, wide)
        pack_ref[:, j : j + wide] = jnp.dot(
            place, v, preferred_element_type=jnp.float32
        ).astype(jnp.bfloat16)


def step(second, where, state, kappa, rate, faces, place):
    levels, rows, cells = state.shape
    slots = place.shape[0]
    ext = (levels, rows + TILE, cells)
    out = [
        jax.ShapeDtypeStruct(state.shape, jnp.float32),
        jax.ShapeDtypeStruct((slots, cells), jnp.bfloat16),
    ]
    if not second:
        out.append(jax.ShapeDtypeStruct((2, levels * TILE // 2, cells), jnp.bfloat16))
    vmem = pl.BlockSpec(memory_space=pltpu.VMEM)
    return pl.pallas_call(
        functools.partial(step_kernel, second),
        out_shape=out,
        in_specs=[pl.BlockSpec(memory_space=pltpu.SMEM)] + [vmem] * (4 + len(faces)),
        out_specs=[vmem] * len(out),
        scratch_shapes=[pltpu.VMEM(ext, jnp.float32) for _ in range(10)],
        compiler_params=pltpu.CompilerParams(vmem_limit_bytes=VMEM),
        cost_estimate=pl.CostEstimate(
            flops=120 * levels * rows * cells, bytes_accessed=22 * levels * rows * cells, transcendentals=0
        ),
    )(where, state, kappa, rate, *faces, place)


def placing(dest, writers, per_dev):
    slots = 2 * per_dev
    capacity = slots // writers
    onehot = (dest == jnp.arange(writers, dtype=jnp.int32)[None, :]).astype(jnp.float32)
    row_ids = jnp.arange(per_dev, dtype=jnp.int32)
    lower = (row_ids[:, None] > row_ids[None, :]).astype(jnp.float32)
    before = jnp.dot(lower, onehot, preferred_element_type=jnp.float32)
    ranks = jnp.sum(before * onehot, axis=1).astype(jnp.int32)
    target = dest[:, 0] * capacity + ranks
    return (jnp.arange(slots, dtype=jnp.int32)[:, None] == target[None, :]).astype(jnp.bfloat16)


def shards(initial, kappa, rate, writer):
    n = lax.axis_size("gx")
    me = lax.axis_index("gx")
    levels, rows, cells = initial.shape
    even = me % 2 == 0
    where = jnp.stack([me % 2, (me < n - 1).astype(jnp.int32), (me > 0).astype(jnp.int32)])
    by_core = [(i, i ^ 1) for i in range(n)]
    by_chip = [(i, i + 1) for i in range(1, n - 1, 2)] + [(i + 1, i) for i in range(1, n - 1, 2)]

    def exchange(top, bottom):
        to_core = jnp.where(even, bottom, top)
        to_chip = jnp.where(even, top, bottom)
        return lax.ppermute(to_core, "gx", by_core), lax.ppermute(to_chip, "gx", by_chip)

    top = jnp.concatenate([initial[:, :3], rate[:, :2], kappa[:, :3]], 1)
    bottom = jnp.concatenate([kappa[:, -3:], rate[:, -2:], initial[:, -3:]], 1)
    flat = (levels * TILE, cells)
    faces = exchange(top.astype(jnp.bfloat16).reshape(flat), bottom.astype(jnp.bfloat16).reshape(flat))
    places = [placing(writer[s], n, levels * rows) for s in range(STEPS)]

    def route(packed):
        return lax.all_to_all(packed, "gx", split_axis=0, concat_axis=0, tiled=True)

    state, packed, edge = step(False, where, initial, kappa, rate, faces, places[0])
    first = route(packed)
    faces = faces + exchange(edge[0], edge[1])
    state, packed = step(True, where, state, kappa, rate, faces, places[1])
    return state, jnp.stack([first, route(packed)])


def solution(mesh):
    spec = P("runs", "gx", None)
    return jax.shard_map(
        shards, mesh=mesh, in_specs=(spec,) * 4, out_specs=(spec, spec), check_vma=False
    )
```

```python
import functools

import jax
import jax.numpy as jnp
from jax import lax
from jax.experimental import pallas as pl
from jax.experimental.pallas import tpu as pltpu
from jax.sharding import PartitionSpec as P

STEPS = 2
DT = 0.15
LANES = 128
TILE = 8
WIDE = 2 * LANES
VMEM = 48 * 1024 * 1024


def roll_rows(v, shift):
    shift = shift % v.shape[0]
    return pltpu.roll(v, shift, 0) if shift else v


def pack_kernel(u_top, k_top, r_top, u_bot, k_bot, r_bot, core_ref, chip_ref):
    levels, _, cells = u_top.shape
    even = lax.axis_index("gx") % 2 == 0
    row = lax.broadcasted_iota(jnp.int32, (TILE, LANES), 0)
    for j in range(0, cells, LANES):
        c = slice(j, j + LANES)
        top, bot = [], []
        last_top = last_bot = jnp.zeros((TILE, LANES), jnp.float32)
        for l in range(levels):
            u, k, r = u_top[l, :, c], k_top[l, :, c], r_top[l, :, c]
            top += [jnp.where(row < 6, u, roll_rows(r, 6)), jnp.where(row < 6, k, roll_rows(r, 4))]
            last_top = jnp.where(row == l, roll_rows(r, l - 4), last_top)
            u, k, r = u_bot[l, :, c], k_bot[l, :, c], r_bot[l, :, c]
            bot += [jnp.where(row >= 2, u, roll_rows(r, 2)), jnp.where(row >= 2, k, roll_rows(r, 4))]
            last_bot = jnp.where(row == l, roll_rows(r, l - 3), last_bot)
        top = jnp.concatenate(top + [last_top], 0).astype(jnp.bfloat16)
        bot = jnp.concatenate(bot + [last_bot], 0).astype(jnp.bfloat16)
        core_ref[:, c] = jnp.where(even, bot, top)
        chip_ref[:, c] = jnp.where(even, top, bot)


def pack_faces(u, k, r):
    levels, rows, cells = u.shape
    top = pl.BlockSpec((levels, TILE, cells), lambda i: (0, 0, 0))
    bot = pl.BlockSpec((levels, TILE, cells), lambda i: (0, rows // TILE - 1, 0))
    shape = ((2 * levels + 1) * TILE, cells)
    out = pl.BlockSpec(shape, lambda i: (0, 0))
    return pl.pallas_call(
        pack_kernel,
        grid=(1,),
        out_shape=[jax.ShapeDtypeStruct(shape, jnp.bfloat16)] * 2,
        in_specs=[top] * 3 + [bot] * 3,
        out_specs=[out] * 2,
        compiler_params=pltpu.CompilerParams(vmem_limit_bytes=16 * 1024 * 1024),
    )(u, k, r, u, k, r)


def step_kernel(first, u_ref, k_ref, r_ref, *refs):
    if first:
        core_ref, chip_ref, place_ref, state_out, pack_out, face_out, face = refs[:7]
        refs = refs[7:]
    else:
        face_ref, place_ref, state_out, pack_out = refs[:4]
        refs = refs[4:]
    u0, u1, u2, xp, xm, yp, ym, zp, lin, quad, new, packed, sems = refs
    levels, rows, cells = u_ref.shape
    ext = u0.shape[1]
    chunks = cells // LANES
    me, n = lax.axis_index("gx"), lax.axis_size("gx")
    even = me % 2 == 0
    row = lax.broadcasted_iota(jnp.int32, (TILE, LANES), 0)
    lane = lax.broadcasted_iota(jnp.int32, (ext, LANES), 1)
    if first:
        side = lax.broadcasted_iota(jnp.int32, (2 * TILE, LANES), 0) < TILE
    else:
        side = row < TILE // 2
    live = jnp.where(side, (me < n - 1).astype(jnp.int32), (me > 0).astype(jnp.int32)) > 0

    def cols(j):
        j = j % chunks
        return slice(j * LANES, (j + 1) * LANES)

    kk = u2
    for j in range(chunks):
        c = cols(j)
        if first:
            core, chip = core_ref[:, c].astype(jnp.float32), chip_ref[:, c].astype(jnp.float32)
            below, above = jnp.where(even, core, chip), jnp.where(even, chip, core)
            last = 2 * levels * TILE
            r_below, r_above = below[last:], above[last:]
        for l in range(levels):
            if first:
                s = 2 * l * TILE
                ub, kb = below[s : s + TILE], below[s + TILE : s + 2 * TILE]
                ua, ka = above[s : s + TILE], above[s + TILE : s + 2 * TILE]
                rb = jnp.where(row < 4, roll_rows(kb, 4), roll_rows(r_below, 4 - l))
                rb = jnp.where(row < 2, roll_rows(ub, 2), rb)
                ra = jnp.where(row >= 4, roll_rows(ka, 4), roll_rows(r_above, 3 - l))
                ra = jnp.where(row >= 6, roll_rows(ua, 6), ra)
                faces = [((rows, ub, kb, rb)), ((rows + TILE, ua, ka, ra))]
                face[1, l, :, c] = jnp.where(row < 4, kb, ka)
                face[2, l, :, c] = jnp.where(row < 4, rb, ra)
            else:
                faces = [(rows, face_ref[0, l, :, c], face_ref[1, l, :, c], face_ref[2, l, :, c])]
            kk[l, :rows, c] = k_ref[l, :, c]
            u0[l, :rows, c] = u_ref[l, :, c]
            quad[l, :rows, c] = DT * r_ref[l, :, c]
            for at, u, k, r in faces:
                u0[l, at : at + TILE, c] = u
                kk[l, at : at + TILE, c] = k
                quad[l, at : at + TILE, c] = DT * r

    def left_right(src, l):
        right, left, here = {}, {}, {}

        def rots(j):
            j = j % chunks
            if j not in here:
                v = src[l, :, cols(j)]
                here[j] = v
                right[j] = pltpu.roll(v, LANES - 1, 1)
                left[j] = pltpu.roll(v, 1, 1)
            return j

        def at(j):
            a, b, d = rots(j - 1), rots(j), rots(j + 1)
            return (
                here[b],
                jnp.where(lane == LANES - 1, right[d], right[b]),
                jnp.where(lane == 0, left[a], left[b]),
            )

        return at

    half = 0.5 * DT
    ats = [left_right(kk, l) for l in range(levels)]
    for j in range(chunks):
        c = cols(j)
        for l in range(levels):
            k, k_right, k_left = ats[l](j)
            a = half * (k + pltpu.roll(k, ext - 1, 0))
            b = pltpu.roll(a, 1, 0)
            d, e = half * (k + k_right), half * (k + k_left)
            xp[l, :, c], xm[l, :, c], yp[l, :, c], ym[l, :, c] = a, b, d, e
            total = a + b + d + e
            if l < levels - 1:
                f = half * (k + kk[l + 1, :, c])
                zp[l, :, c] = f
                total = total + f
            if l > 0:
                total = total + zp[l - 1, :, c]
            lin[l, :, c] = 1.0 + quad[l, :, c] - total

    def euler(src, ats, l, j):
        c = cols(j)
        u, u_right, u_left = ats[l](j)
        out = u * (lin[l, :, c] - quad[l, :, c] * u)
        out = out + xp[l, :, c] * pltpu.roll(u, ext - 1, 0) + xm[l, :, c] * pltpu.roll(u, 1, 0)
        out = out + yp[l, :, c] * u_right + ym[l, :, c] * u_left
        if l < levels - 1:
            out = out + zp[l, :, c] * src[l + 1, :, c]
        if l > 0:
            out = out + zp[l - 1, :, c] * src[l - 1, :, c]
        return out

    def masked(dst, l, c, v):
        dst[l, :rows, c] = v[:rows]
        dst[l, rows:, c] = jnp.where(live, v[rows:], 0.0)

    ats = [left_right(u0, l) for l in range(levels)]
    for j in range(chunks):
        for l in range(levels):
            masked(u1, l, cols(j), euler(u0, ats, l, j))
    ats = [left_right(u1, l) for l in range(levels)]
    for j in range(chunks):
        for l in range(levels):
            c = cols(j)
            masked(u2, l, c, 0.75 * u0[l, :, c] + 0.25 * euler(u1, ats, l, j))
    ats = [left_right(u2, l) for l in range(levels)]
    place = place_ref[...]
    copies = []

    def send(src, dst):
        copy = pltpu.make_async_copy(src, dst, sems.at[len(copies)])
        copy.start()
        copies.append(copy)

    per = WIDE // LANES
    for j in range(chunks):
        for l in range(levels):
            c = cols(j)
            v = (1.0 / 3.0) * u0[l, :, c] + (2.0 / 3.0) * euler(u2, ats, l, j)
            new[l, :, c] = v[:rows]
            if first:
                v = jnp.where(live, v[rows:], 0.0)
                face[0, l, :, c] = jnp.where(
                    row < 3, v[:TILE], jnp.where(row < 5, 0.0, v[TILE:])
                )
        if j % per == per - 1:
            c = slice((j + 1) * LANES - WIDE, (j + 1) * LANES)
            v = new[:, :, c].astype(jnp.bfloat16).reshape(levels * rows, WIDE)
            packed[:, c] = jnp.dot(place, v, preferred_element_type=jnp.float32).astype(
                jnp.bfloat16
            )
            send(packed.at[:, c], pack_out.at[:, c])
            send(new.at[:, :, c], state_out.at[:, :, c])
    if first:
        send(face, face_out)
    for copy in copies:
        copy.wait()


def step(first, state, kappa, rate, faces, place):
    levels, rows, cells = state.shape
    slots = place.shape[0]
    ext = (levels, rows + (2 * TILE if first else TILE), cells)
    out = [
        jax.ShapeDtypeStruct(state.shape, jnp.float32),
        jax.ShapeDtypeStruct((slots, cells), jnp.bfloat16),
    ]
    scratch = [pltpu.VMEM(ext, jnp.float32) for _ in range(10)] + [
        pltpu.VMEM(state.shape, jnp.float32),
        pltpu.VMEM((slots, cells), jnp.bfloat16),
        pltpu.SemaphoreType.DMA((2 * (cells // WIDE) + 1,)),
    ]
    if first:
        face = (3, levels, TILE, cells)
        out.append(jax.ShapeDtypeStruct(face, jnp.float32))
        scratch.insert(0, pltpu.VMEM(face, jnp.float32))
    return pl.pallas_call(
        functools.partial(step_kernel, first),
        out_shape=out,
        in_specs=[pl.BlockSpec(memory_space=pltpu.VMEM)] * (4 + len(faces)),
        out_specs=[pl.BlockSpec(memory_space=pltpu.HBM)] * len(out),
        scratch_shapes=scratch,
        compiler_params=pltpu.CompilerParams(vmem_limit_bytes=VMEM),
        cost_estimate=pl.CostEstimate(
            flops=120 * levels * rows * cells,
            bytes_accessed=22 * levels * rows * cells,
            transcendentals=0,
        ),
    )(state, kappa, rate, *faces, place)


def put_kernel(at, part_ref, *refs):
    out_ref, sem = refs[-2:]
    copy = pltpu.make_async_copy(part_ref, out_ref.at[at], sem)
    copy.start()
    copy.wait()


def put(at, part, whole=None):
    args = (part,) if whole is None else (part, whole)
    return pl.pallas_call(
        functools.partial(put_kernel, at),
        out_shape=jax.ShapeDtypeStruct((STEPS, *part.shape), part.dtype),
        in_specs=[pl.BlockSpec(memory_space=pl.ANY)] * len(args),
        out_specs=pl.BlockSpec(memory_space=pltpu.HBM),
        scratch_shapes=[pltpu.SemaphoreType.DMA],
        input_output_aliases={} if whole is None else {1: 0},
    )(*args)


def placing(dest, writers, per_dev):
    slots = 2 * per_dev
    capacity = slots // writers
    onehot = (dest == jnp.arange(writers, dtype=jnp.int32)[None, :]).astype(jnp.float32)
    row_ids = jnp.arange(per_dev, dtype=jnp.int32)
    lower = (row_ids[:, None] > row_ids[None, :]).astype(jnp.float32)
    before = jnp.dot(lower, onehot, preferred_element_type=jnp.float32)
    ranks = jnp.sum(before * onehot, axis=1).astype(jnp.int32)
    target = dest[:, 0] * capacity + ranks
    return (jnp.arange(slots, dtype=jnp.int32)[:, None] == target[None, :]).astype(jnp.bfloat16)


def shards(initial, kappa, rate, writer):
    n = lax.axis_size("gx")
    levels, rows, cells = initial.shape
    by_core = [(i, i ^ 1) for i in range(n)]
    by_chip = [(i, i + 1) for i in range(1, n - 1, 2)] + [(i + 1, i) for i in range(1, n - 1, 2)]
    to_core, to_chip = pack_faces(initial, kappa, rate)
    faces = (lax.ppermute(to_core, "gx", by_core), lax.ppermute(to_chip, "gx", by_chip))
    places = [placing(writer[s], n, levels * rows) for s in range(STEPS)]

    def route(packed):
        return lax.all_to_all(packed, "gx", split_axis=0, concat_axis=0, tiled=True)

    state, packed, face = step(True, initial, kappa, rate, faces, places[0])
    first = route(packed)
    state, packed = step(False, state, kappa, rate, (face,), places[1])
    second = route(packed)
    return state, put(1, second, put(0, first))


def solution(mesh):
    spec = P("runs", "gx", None)
    return jax.shard_map(
        shards, mesh=mesh, in_specs=(spec,) * 4, out_specs=(spec, spec), check_vma=False
    )
```

```python
import functools

import jax
import jax.numpy as jnp
from jax import lax
from jax.experimental import pallas as pl
from jax.experimental.pallas import tpu as pltpu
from jax.sharding import PartitionSpec as P

STEPS = 2
DT = 0.15
LANES = 128
TILE = 8
WIDE = 2 * LANES
VMEM = 30 * 1024 * 1024


def roll_rows(v, shift):
    shift = shift % v.shape[0]
    return pltpu.roll(v, shift, 0) if shift else v


def pack_kernel(u_ref, k_ref, r_ref, core_ref, chip_ref, deep_ref, top, bot, sems):
    levels, rows, cells = u_ref.shape
    copies = []
    for i, ref in enumerate((u_ref, k_ref, r_ref)):
        copies.append(pltpu.make_async_copy(ref.at[:, :TILE], top.at[i], sems.at[0, i]))
        copies.append(pltpu.make_async_copy(ref.at[:, rows - TILE :], bot.at[i], sems.at[1, i]))
    for copy in copies:
        copy.start()
    for copy in copies:
        copy.wait()
    even = lax.axis_index("gx") % 2 == 0
    row = lax.broadcasted_iota(jnp.int32, (TILE, LANES), 0)
    near = levels * TILE
    for j in range(0, cells, LANES):
        c = slice(j, j + LANES)
        first, last, deep_first, deep_last = [], [], [], []
        end_first = end_last = zero = jnp.zeros((TILE, LANES), jnp.float32)
        for l in range(levels):
            u, k, r = top[0, l, :, c], top[1, l, :, c], top[2, l, :, c]
            k5 = roll_rows(k, 5)
            first.append(jnp.where(row < 3, u, jnp.where(row < 5, roll_rows(r, 3), k5)))
            v = jnp.where(row < 3, k5, roll_rows(r, 4))
            deep_first.append(jnp.where((row < 3) | (row >= 6), v, u))
            end_first = jnp.where(row == l, roll_rows(r, l - 4), end_first)
            u, k, r = bot[0, l, :, c], bot[1, l, :, c], bot[2, l, :, c]
            k3 = roll_rows(k, 3)
            last.append(jnp.where(row < 5, jnp.where(row < 3, k3, roll_rows(r, 5)), u))
            v = jnp.where(row < 2, roll_rows(r, 4), k3)
            deep_last.append(jnp.where((row < 2) | (row >= 5), v, u))
            end_last = jnp.where(row == l, roll_rows(r, l - 3), end_last)
        a = jnp.concatenate(first + deep_first + [end_first, zero], 0)
        b = jnp.concatenate(last + deep_last + [end_last, zero], 0)
        core_ref[:, c] = jnp.where(even, b, a).astype(jnp.bfloat16)
        chip = jnp.where(even, a, b).astype(jnp.bfloat16)
        chip_ref[:, c] = chip[:near]
        deep_ref[:, c] = chip[near : near + deep_ref.shape[0]]


def pack_faces(u, k, r):
    levels, _, cells = u.shape
    hbm = pl.BlockSpec(memory_space=pltpu.HBM)
    sizes = [(2 * levels + 2) * TILE, levels * TILE, (levels + 2) * TILE]
    return pl.pallas_call(
        pack_kernel,
        out_shape=[jax.ShapeDtypeStruct((size, cells), jnp.bfloat16) for size in sizes],
        in_specs=[hbm] * 3,
        out_specs=[pl.BlockSpec(memory_space=pltpu.VMEM)] * 3,
        scratch_shapes=[pltpu.VMEM((3, levels, TILE, cells), jnp.float32)] * 2
        + [pltpu.SemaphoreType.DMA((2, 3))],
        compiler_params=pltpu.CompilerParams(vmem_limit_bytes=60 * 1024 * 1024),
    )(u, k, r)


def sections(shape, fill, live, done, u0, u1, u2, xp, xm, yp, ym, zp, lin, quad):
    levels, ext, cells = shape
    chunks = cells // LANES
    lane = lax.broadcasted_iota(jnp.int32, (ext, LANES), 1)

    def cols(j):
        j = j % chunks
        return slice(j * LANES, (j + 1) * LANES)

    kk = u2

    def left_right(src, l):
        right, left, here = {}, {}, {}

        def rots(j):
            j = j % chunks
            if j not in here:
                v = src[l, :, cols(j)]
                here[j] = v
                right[j] = pltpu.roll(v, LANES - 1, 1)
                left[j] = pltpu.roll(v, 1, 1)
            return j

        def at(j):
            a, b, d = rots(j - 1), rots(j), rots(j + 1)
            return (
                here[b],
                jnp.where(lane == LANES - 1, right[d], right[b]),
                jnp.where(lane == 0, left[a], left[b]),
            )

        return at

    half = 0.5 * DT
    ats = [left_right(kk, l) for l in range(levels)]
    filled = set()
    for j in range(chunks):
        for i in (j - 1, j, j + 1):
            if i % chunks not in filled:
                filled.add(i % chunks)
                fill(i % chunks, u0, kk, quad)
        c = cols(j)
        for l in range(levels):
            k, k_right, k_left = ats[l](j)
            a = half * (k + pltpu.roll(k, ext - 1, 0))
            b = pltpu.roll(a, 1, 0)
            d, e = half * (k + k_right), half * (k + k_left)
            xp[l, :, c], xm[l, :, c], yp[l, :, c], ym[l, :, c] = a, b, d, e
            total = a + b + d + e
            if l < levels - 1:
                f = half * (k + kk[l + 1, :, c])
                zp[l, :, c] = f
                total = total + f
            if l > 0:
                total = total + zp[l - 1, :, c]
            q = DT * quad[l, :, c]
            quad[l, :, c] = q
            lin[l, :, c] = 1.0 + q - total

    def euler(src, ats, l, j):
        c = cols(j)
        u, u_right, u_left = ats[l](j)
        out = u * (lin[l, :, c] - quad[l, :, c] * u)
        out = out + xp[l, :, c] * pltpu.roll(u, ext - 1, 0) + xm[l, :, c] * pltpu.roll(u, 1, 0)
        out = out + yp[l, :, c] * u_right + ym[l, :, c] * u_left
        if l < levels - 1:
            out = out + zp[l, :, c] * src[l + 1, :, c]
        if l > 0:
            out = out + zp[l - 1, :, c] * src[l - 1, :, c]
        return out

    def masked(dst, l, c, v):
        at = 0
        for start, stop, keep in live:
            if at < start:
                dst[l, at:start, c] = v[at:start]
            dst[l, start:stop, c] = jnp.where(keep, v[start:stop], 0.0)
            at = stop
        if at < ext:
            dst[l, at:, c] = v[at:]

    ats = [left_right(u0, l) for l in range(levels)]
    for j in range(chunks):
        for l in range(levels):
            masked(u1, l, cols(j), euler(u0, ats, l, j))
    ats = [left_right(u1, l) for l in range(levels)]
    for j in range(chunks):
        for l in range(levels):
            c = cols(j)
            masked(u2, l, c, 0.75 * u0[l, :, c] + 0.25 * euler(u1, ats, l, j))
    ats = [left_right(u2, l) for l in range(levels)]
    for j in range(chunks):
        c = cols(j)
        done(
            c,
            [
                (1.0 / 3.0) * u0[l, :, c] + (2.0 / 3.0) * euler(u2, ats, l, j)
                for l in range(levels)
            ],
        )


def grid_ends():
    me, n = lax.axis_index("gx"), lax.axis_size("gx")
    return (me < n - 1).astype(jnp.int32), (me > 0).astype(jnp.int32), me % 2 == 0


def sides(core, chip, even):
    core, chip = core.astype(jnp.float32), chip.astype(jnp.float32)
    return jnp.where(even, core, chip), jnp.where(even, chip, core)


def step_kernel(first, u_ref, k_ref, r_ref, core_ref, chip_ref, *refs):
    face_ref = None if first else refs[0]
    place_ref, state_out, *outs = refs[0 if first else 1 : -14]
    scratch, (new, packed, got, sems) = refs[-14:-4], refs[-4:]
    levels, rows, cells = u_ref.shape
    after, before, even = grid_ends()
    row = lax.broadcasted_iota(jnp.int32, (TILE, LANES), 0)
    side = row < TILE // 2
    per = WIDE // LANES
    groups = cells // WIDE
    u0, kk, quad = scratch[0], scratch[2], scratch[9]
    loads = {}
    for g in (groups - 1, *range(groups - 1)):
        c = slice(g * WIDE, (g + 1) * WIDE)
        loads[g] = [
            pltpu.make_async_copy(ref.at[:, :, c], to.at[:, :rows, c], got.at[i, g])
            for i, (ref, to) in enumerate(((k_ref, kk), (u_ref, u0), (r_ref, quad)))
        ]
        for load in loads[g]:
            load.start()

    def fill(j, u0, kk, quad):
        for load in loads.pop(j // per, ()):
            load.wait()
        c = slice(j * LANES, (j + 1) * LANES)
        near = levels * TILE
        below, above = sides(core_ref[:near, c], chip_ref[:, c], even)
        for l in range(levels):
            b, a = below[l * TILE : (l + 1) * TILE], above[l * TILE : (l + 1) * TILE]
            u0[l, rows:, c] = jnp.where(side, b, a) if first else face_ref[l, :, c]
            kk[l, rows:, c] = jnp.where(side, roll_rows(b, 3), roll_rows(a, 5))
            quad[l, rows:, c] = jnp.where(side, roll_rows(b, 5), roll_rows(a, 3))

    place = place_ref[...]
    copies = []

    def send(src, dst):
        copy = pltpu.make_async_copy(src, dst, sems.at[len(copies)])
        copy.start()
        copies.append(copy)

    def done(c, values):
        for l, v in enumerate(values):
            new[l, :, c] = v[:rows]
        if c.stop % WIDE == 0:
            c = slice(c.stop - WIDE, c.stop)
            send(new.at[:, :, c], state_out.at[:, :, c])
            v = new[:, :, c].astype(jnp.bfloat16).reshape(levels * rows, WIDE)
            v = jnp.dot(place, v, preferred_element_type=jnp.float32).astype(jnp.bfloat16)
            if first:
                packed[:, c] = v
                send(packed.at[:, c], outs[0].at[:, c])
            else:
                at = 0
                for out in outs:
                    out[:, c] = v[at : at + out.shape[0]]
                    at += out.shape[0]

    live = [(rows, rows + TILE, jnp.where(side, after, before) > 0)]
    sections((levels, rows + TILE, cells), fill, live, done, *scratch)
    for copy in copies:
        copy.wait()


def strip_kernel(u_ref, k_ref, r_ref, core_ref, chip_ref, deep_ref, face_ref, *refs):
    scratch, top, bot, sems = refs[:10], refs[10], refs[11], refs[12]
    levels, rows, cells = u_ref.shape
    copies = []
    for i, ref in enumerate((u_ref, k_ref, r_ref)):
        copies.append(pltpu.make_async_copy(ref.at[:, :TILE], top.at[i], sems.at[0, i]))
        copies.append(pltpu.make_async_copy(ref.at[:, rows - TILE :], bot.at[i], sems.at[1, i]))
    for copy in copies:
        copy.start()
    for copy in copies:
        copy.wait()
    after, before, even = grid_ends()
    row = lax.broadcasted_iota(jnp.int32, (TILE, LANES), 0)

    def fill(j, u0, kk, quad):
        c = slice(j * LANES, (j + 1) * LANES)
        near = levels * TILE
        below, above = sides(core_ref[:near, c], chip_ref[:, c], even)
        below2, above2 = sides(core_ref[near:, c], deep_ref[:, c], even)
        r_below, r_above = below2[near : near + TILE], above2[near : near + TILE]
        for l in range(levels):
            t = slice(l * TILE, (l + 1) * TILE)
            b, a, b2, a2 = below[t], above[t], below2[t], above2[t]
            rb = jnp.where(row < 4, roll_rows(b2, 4), roll_rows(r_below, 4 - l))
            ra = jnp.where(row >= 4, roll_rows(a2, 4), roll_rows(r_above, 3 - l))
            for at, u, k, r in (
                (0, bot[0, l, :, c], bot[1, l, :, c], bot[2, l, :, c]),
                (
                    TILE,
                    jnp.where(row < 3, b, b2),
                    roll_rows(jnp.where(row >= 5, b, b2), 3),
                    jnp.where(row < 2, roll_rows(b, 5), rb),
                ),
                (
                    2 * TILE,
                    jnp.where(row >= 5, a, a2),
                    roll_rows(jnp.where(row < 3, a, a2), 5),
                    jnp.where(row >= 6, roll_rows(a, 3), ra),
                ),
                (3 * TILE, top[0, l, :, c], top[1, l, :, c], top[2, l, :, c]),
            ):
                u0[l, at : at + TILE, c] = u
                kk[l, at : at + TILE, c] = k
                quad[l, at : at + TILE, c] = r

    keep_after = jnp.where(row < TILE, after, 0) > 0
    keep_before = jnp.where(row < TILE, before, 0) > 0

    def done(c, values):
        for l, v in enumerate(values):
            b = jnp.where(keep_after, v[TILE : 2 * TILE], 0.0)
            a = jnp.where(keep_before, v[2 * TILE : 3 * TILE], 0.0)
            face_ref[l, :, c] = jnp.where(row < 3, b, jnp.where(row < 5, 0.0, a))

    live = [(TILE, 2 * TILE, keep_after), (2 * TILE, 3 * TILE, keep_before)]
    sections((levels, 4 * TILE, cells), fill, live, done, *scratch)


def strip(u, k, r, packets):
    levels, _, cells = u.shape
    hbm, vmem = pl.BlockSpec(memory_space=pltpu.HBM), pl.BlockSpec(memory_space=pltpu.VMEM)
    return pl.pallas_call(
        strip_kernel,
        out_shape=jax.ShapeDtypeStruct((levels, TILE, cells), jnp.float32),
        in_specs=[hbm] * 3 + [vmem] * 3,
        out_specs=vmem,
        scratch_shapes=[pltpu.VMEM((levels, 4 * TILE, cells), jnp.float32)] * 10
        + [pltpu.VMEM((3, levels, TILE, cells), jnp.float32)] * 2
        + [pltpu.SemaphoreType.DMA((2, 3))],
        compiler_params=pltpu.CompilerParams(vmem_limit_bytes=VMEM),
        cost_estimate=pl.CostEstimate(
            flops=100 * levels * 4 * TILE * cells,
            bytes_accessed=22 * levels * 4 * TILE * cells,
            transcendentals=0,
        ),
    )(u, k, r, *packets)


def step(first, state, kappa, rate, faces, place, parts, limit):
    levels, rows, cells = state.shape
    slots = place.shape[0]
    out = [jax.ShapeDtypeStruct(state.shape, jnp.float32)]
    out += [jax.ShapeDtypeStruct((slots // parts, cells), jnp.bfloat16)] * parts
    vmem, hbm = pl.BlockSpec(memory_space=pltpu.VMEM), pl.BlockSpec(memory_space=pltpu.HBM)
    groups = cells // WIDE
    return pl.pallas_call(
        functools.partial(step_kernel, first),
        out_shape=out,
        in_specs=[hbm] * 3 + [vmem] * (1 + len(faces)),
        out_specs=[hbm] + [hbm if first else vmem] * parts,
        scratch_shapes=[pltpu.VMEM((levels, rows + TILE, cells), jnp.float32)] * 10
        + [
            pltpu.VMEM(state.shape, jnp.float32),
            pltpu.VMEM((slots, cells) if first else (16, LANES), jnp.bfloat16),
            pltpu.SemaphoreType.DMA((3, groups)),
            pltpu.SemaphoreType.DMA((2 * groups,)),
        ],
        compiler_params=pltpu.CompilerParams(vmem_limit_bytes=limit * 1024 * 1024),
        cost_estimate=pl.CostEstimate(
            flops=120 * levels * rows * cells,
            bytes_accessed=22 * levels * rows * cells,
            transcendentals=0,
        ),
    )(state, kappa, rate, *faces, place)


def vmem_call(kernel, args, out, **kw):
    vmem = pl.BlockSpec(memory_space=pltpu.VMEM)
    return pl.pallas_call(
        kernel,
        out_shape=out,
        in_specs=kw.pop("in_specs", [vmem] * len(args)),
        out_specs=kw.pop("out_specs", [vmem] * len(out)),
        compiler_params=pltpu.CompilerParams(vmem_limit_bytes=16 * 1024 * 1024),
        **kw,
    )(*args)


def weave_kernel(mine_ref, theirs_ref, *outs):
    odd = lax.axis_index("gx") % 2 == 1
    size = outs[0].shape[0] // 2
    for p, out in enumerate(outs):
        a, b = mine_ref[p * size : (p + 1) * size], theirs_ref[p * size : (p + 1) * size]
        out[:size] = jnp.where(odd, b, a)
        out[size:] = jnp.where(odd, a, b)


def put_kernel(part_ref, out_ref, sem):
    copy = pltpu.make_async_copy(part_ref, out_ref.at[0], sem)
    copy.start()
    copy.wait()


def put_blocks_kernel(which, *refs):
    blocks, out_ref, sems = refs[: len(which)], refs[-2], refs[-1]
    chip = lax.axis_index("gx") // 2
    copies = []
    for i, (p, ref) in enumerate(zip(which, blocks, strict=True)):
        size = ref.shape[0]
        at = pl.multiple_of((chip ^ p) * size, size)
        copies.append(
            pltpu.make_async_copy(ref, out_ref.at[1, pl.ds(at, size)], sems.at[i])
        )
    for copy in copies:
        copy.start()
    for copy in copies:
        copy.wait()


def placing(dest, block_of, writers, per_dev):
    slots = 2 * per_dev
    capacity = slots // writers
    onehot = (dest == jnp.arange(writers, dtype=jnp.int32)[None, :]).astype(jnp.float32)
    row_ids = jnp.arange(per_dev, dtype=jnp.int32)
    lower = (row_ids[:, None] > row_ids[None, :]).astype(jnp.float32)
    before = jnp.dot(lower, onehot, preferred_element_type=jnp.float32)
    ranks = jnp.sum(before * onehot, axis=1).astype(jnp.int32)
    target = block_of(dest[:, 0]) * capacity + ranks
    return (jnp.arange(slots, dtype=jnp.int32)[:, None] == target[None, :]).astype(jnp.bfloat16)


def shards(initial, kappa, rate, writer):
    n = lax.axis_size("gx")
    levels, rows, cells = initial.shape
    per_dev = levels * rows
    slots = 2 * per_dev
    capacity = slots // n
    by_core = [(i, i ^ 1) for i in range(n)]
    by_chip = [(i, i + 1) for i in range(1, n - 1, 2)] + [(i + 1, i) for i in range(1, n - 1, 2)]

    def route(packed):
        return lax.all_to_all(packed, "gx", split_axis=0, concat_axis=0, tiled=True)

    to_core, to_chip, deep = pack_faces(initial, kappa, rate)
    faces = [lax.ppermute(to_core, "gx", by_core), lax.ppermute(to_chip, "gx", by_chip)]
    deep = lax.ppermute(deep, "gx", by_chip)
    place = placing(writer[0], lambda d: d, n, per_dev)
    state, packed = step(True, initial, kappa, rate, faces, place, 1, 53)
    packed, deep = lax.optimization_barrier((packed, deep))
    first = route(packed)
    faces = faces + [strip(initial, kappa, rate, faces + [deep])]
    if capacity % 16 or n & (n - 1):
        place = placing(writer[1], lambda d: d, n, per_dev)
        state, packed = step(False, state, kappa, rate, faces, place, 1, 30)
        return state, jnp.stack([first, route(packed)])

    chips = n // 2
    me = lax.axis_index("gx")
    place = placing(writer[1], lambda d: ((d ^ me) & 1) * chips + ((d ^ me) >> 1), n, per_dev)
    state, mine, theirs = step(False, state, kappa, rate, faces, place, 2, 30)
    theirs = lax.ppermute(theirs, "gx", by_core)
    block = jax.ShapeDtypeStruct((2 * capacity, cells), jnp.bfloat16)
    frames = jax.ShapeDtypeStruct((STEPS, slots, cells), jnp.bfloat16)
    hbm = pl.BlockSpec(memory_space=pltpu.HBM)
    vmem = pl.BlockSpec(memory_space=pltpu.VMEM)
    blocks = vmem_call(weave_kernel, (mine, theirs), [block] * chips)
    got = [blocks[0]]
    for p in range(1, chips):
        got.append(lax.ppermute(blocks[p], "gx", [(i, i ^ (2 * p)) for i in range(n)]))
    (out,) = vmem_call(
        put_kernel,
        (first,),
        [frames],
        out_specs=[hbm],
        scratch_shapes=[pltpu.SemaphoreType.DMA],
    )
    (out,) = vmem_call(
        functools.partial(put_blocks_kernel, range(chips)),
        (*got, out),
        [frames],
        in_specs=[vmem] * chips + [hbm],
        out_specs=[hbm],
        scratch_shapes=[pltpu.SemaphoreType.DMA((chips,))],
        input_output_aliases={chips: 0},
    )
    return state, out


def solution(mesh):
    spec = P("runs", "gx", None)
    return jax.shard_map(
        shards, mesh=mesh, in_specs=(spec,) * 4, out_specs=(spec, spec), check_vma=False
    )
```

```python
import functools

import jax
import jax.numpy as jnp
from jax import lax
from jax.experimental import pallas as pl
from jax.experimental.pallas import tpu as pltpu
from jax.sharding import PartitionSpec as P

STEPS = 2
DT = 0.15
LANES = 128
TILE = 8
WIDE = 2 * LANES
VMEM = 30 * 1024 * 1024


def roll_rows(v, shift):
    shift = shift % v.shape[0]
    return pltpu.roll(v, shift, 0) if shift else v


def pack_kernel(u_ref, k_ref, r_ref, core_ref, chip_ref, deep_ref, top, bot, sems):
    levels, rows, cells = u_ref.shape
    copies = []
    for i, ref in enumerate((u_ref, k_ref, r_ref)):
        copies.append(pltpu.make_async_copy(ref.at[:, :TILE], top.at[i], sems.at[0, i]))
        copies.append(pltpu.make_async_copy(ref.at[:, rows - TILE :], bot.at[i], sems.at[1, i]))
    for copy in copies:
        copy.start()
    for copy in copies:
        copy.wait()
    even = lax.axis_index("gx") % 2 == 0
    row = lax.broadcasted_iota(jnp.int32, (TILE, LANES), 0)
    near = levels * TILE
    for j in range(0, cells, LANES):
        c = slice(j, j + LANES)
        first, last, deep_first, deep_last = [], [], [], []
        end_first = end_last = zero = jnp.zeros((TILE, LANES), jnp.float32)
        for l in range(levels):
            u, k, r = top[0, l, :, c], top[1, l, :, c], top[2, l, :, c]
            k5 = roll_rows(k, 5)
            first.append(jnp.where(row < 3, u, jnp.where(row < 5, roll_rows(r, 3), k5)))
            v = jnp.where(row < 3, k5, roll_rows(r, 4))
            deep_first.append(jnp.where((row < 3) | (row >= 6), v, u))
            end_first = jnp.where(row == l, roll_rows(r, l - 4), end_first)
            u, k, r = bot[0, l, :, c], bot[1, l, :, c], bot[2, l, :, c]
            k3 = roll_rows(k, 3)
            last.append(jnp.where(row < 5, jnp.where(row < 3, k3, roll_rows(r, 5)), u))
            v = jnp.where(row < 2, roll_rows(r, 4), k3)
            deep_last.append(jnp.where((row < 2) | (row >= 5), v, u))
            end_last = jnp.where(row == l, roll_rows(r, l - 3), end_last)
        a = jnp.concatenate(first + deep_first + [end_first, zero], 0)
        b = jnp.concatenate(last + deep_last + [end_last, zero], 0)
        core_ref[:, c] = jnp.where(even, b, a).astype(jnp.bfloat16)
        chip = jnp.where(even, a, b).astype(jnp.bfloat16)
        chip_ref[:, c] = chip[:near]
        deep_ref[:, c] = chip[near : near + deep_ref.shape[0]]


def pack_faces(u, k, r):
    levels, _, cells = u.shape
    hbm = pl.BlockSpec(memory_space=pltpu.HBM)
    sizes = [(2 * levels + 2) * TILE, levels * TILE, (levels + 2) * TILE]
    return pl.pallas_call(
        pack_kernel,
        out_shape=[jax.ShapeDtypeStruct((size, cells), jnp.bfloat16) for size in sizes],
        in_specs=[hbm] * 3,
        out_specs=[pl.BlockSpec(memory_space=pltpu.VMEM)] * 3,
        scratch_shapes=[pltpu.VMEM((3, levels, TILE, cells), jnp.float32)] * 2
        + [pltpu.SemaphoreType.DMA((2, 3))],
        compiler_params=pltpu.CompilerParams(vmem_limit_bytes=60 * 1024 * 1024),
    )(u, k, r)


def sections(steps, shape, fill, live, done, u0, u1, u2, xp, xm, yp, ym, zp, lin, quad):
    levels, ext, cells = shape
    chunks = cells // LANES
    lane = lax.broadcasted_iota(jnp.int32, (ext, LANES), 1)

    def cols(j):
        j = j % chunks
        return slice(j * LANES, (j + 1) * LANES)

    kk = u2

    def left_right(src, l):
        right, left, here = {}, {}, {}

        def rots(j):
            j = j % chunks
            if j not in here:
                v = src[l, :, cols(j)]
                here[j] = v
                right[j] = pltpu.roll(v, LANES - 1, 1)
                left[j] = pltpu.roll(v, 1, 1)
            return j

        def at(j):
            a, b, d = rots(j - 1), rots(j), rots(j + 1)
            return (
                here[b],
                jnp.where(lane == LANES - 1, right[d], right[b]),
                jnp.where(lane == 0, left[a], left[b]),
            )

        return at

    half = 0.5 * DT
    ats = [left_right(kk, l) for l in range(levels)]
    filled = set()
    for j in range(chunks):
        for i in (j - 1, j, j + 1):
            if i % chunks not in filled:
                filled.add(i % chunks)
                fill(i % chunks, u0, kk, quad)
        c = cols(j)
        for l in range(levels):
            k, k_right, k_left = ats[l](j)
            a = half * (k + pltpu.roll(k, ext - 1, 0))
            b = pltpu.roll(a, 1, 0)
            d, e = half * (k + k_right), half * (k + k_left)
            xp[l, :, c], xm[l, :, c], yp[l, :, c], ym[l, :, c] = a, b, d, e
            total = a + b + d + e
            if l < levels - 1:
                f = half * (k + kk[l + 1, :, c])
                zp[l, :, c] = f
                total = total + f
            if l > 0:
                total = total + zp[l - 1, :, c]
            q = DT * quad[l, :, c]
            quad[l, :, c] = q
            lin[l, :, c] = 1.0 + q - total

    def euler(src, ats, l, j):
        c = cols(j)
        u, u_right, u_left = ats[l](j)
        out = u * (lin[l, :, c] - quad[l, :, c] * u)
        out = out + xp[l, :, c] * pltpu.roll(u, ext - 1, 0) + xm[l, :, c] * pltpu.roll(u, 1, 0)
        out = out + yp[l, :, c] * u_right + ym[l, :, c] * u_left
        if l < levels - 1:
            out = out + zp[l, :, c] * src[l + 1, :, c]
        if l > 0:
            out = out + zp[l - 1, :, c] * src[l - 1, :, c]
        return out

    def masked(dst, l, c, v):
        at = 0
        for start, stop, keep in live:
            if at < start:
                dst[l, at:start, c] = v[at:start]
            dst[l, start:stop, c] = jnp.where(keep, v[start:stop], 0.0)
            at = stop
        if at < ext:
            dst[l, at:, c] = v[at:]

    for step in range(steps):
        ats = [left_right(u0, l) for l in range(levels)]
        for j in range(chunks):
            for l in range(levels):
                masked(u1, l, cols(j), euler(u0, ats, l, j))
        ats = [left_right(u1, l) for l in range(levels)]
        for j in range(chunks):
            for l in range(levels):
                c = cols(j)
                masked(u2, l, c, 0.75 * u0[l, :, c] + 0.25 * euler(u1, ats, l, j))
        ats = [left_right(u2, l) for l in range(levels)]
        for j in range(chunks):
            c = cols(j)
            values = [
                (1.0 / 3.0) * u0[l, :, c] + (2.0 / 3.0) * euler(u2, ats, l, j)
                for l in range(levels)
            ]
            if step == steps - 1:
                done(c, values)
            else:
                for l in range(levels):
                    masked(u0, l, c, values[l])


def grid_ends():
    me, n = lax.axis_index("gx"), lax.axis_size("gx")
    return (me < n - 1).astype(jnp.int32), (me > 0).astype(jnp.int32), me % 2 == 0


def sides(core, chip, even):
    core, chip = core.astype(jnp.float32), chip.astype(jnp.float32)
    return jnp.where(even, core, chip), jnp.where(even, chip, core)


def steps_kernel(steps, u_ref, k_ref, r_ref, core_ref, chip_ref, *refs):
    scratch, refs = refs[-10:], refs[:-10]
    if steps == 1:
        place_ref, *outs, new = refs
    else:
        deep_ref, place_ref, new, *outs = refs
    levels, rows, cells = u_ref.shape
    near = levels * TILE
    after, before, even = grid_ends()
    row = lax.broadcasted_iota(jnp.int32, (TILE, LANES), 0)
    side = row < TILE // 2

    def faces(c):
        below, above = sides(core_ref[:near, c], chip_ref[:, c], even)
        tiles = [slice(l * TILE, (l + 1) * TILE) for l in range(levels)]
        if steps == 1:
            for t in tiles:
                b, a = below[t], above[t]
                yield [
                    (
                        jnp.where(side, b, a),
                        jnp.where(side, roll_rows(b, 3), roll_rows(a, 5)),
                        jnp.where(side, roll_rows(b, 5), roll_rows(a, 3)),
                    )
                ]
            return
        below2, above2 = sides(core_ref[near:, c], deep_ref[:, c], even)
        r_below, r_above = below2[near : near + TILE], above2[near : near + TILE]
        for l, t in enumerate(tiles):
            b, a, b2, a2 = below[t], above[t], below2[t], above2[t]
            rb = jnp.where(row < 4, roll_rows(b2, 4), roll_rows(r_below, 4 - l))
            ra = jnp.where(row >= 4, roll_rows(a2, 4), roll_rows(r_above, 3 - l))
            b_tiles = (
                jnp.where(row < 3, b, b2),
                roll_rows(jnp.where(row >= 5, b, b2), 3),
                jnp.where(row < 2, roll_rows(b, 5), rb),
            )
            a_tiles = (
                jnp.where(row >= 5, a, a2),
                roll_rows(jnp.where(row < 3, a, a2), 5),
                jnp.where(row >= 6, roll_rows(a, 3), ra),
            )
            yield [
                [jnp.where(row < 6, v, 0.0) for v in b_tiles],
                [jnp.where(row >= 2, v, 0.0) for v in a_tiles],
            ]

    def fill(j, u0, kk, quad):
        c = slice(j * LANES, (j + 1) * LANES)
        for l, tiles in enumerate(faces(c)):
            u0[l, :rows, c] = u_ref[l, :, c]
            kk[l, :rows, c] = k_ref[l, :, c]
            quad[l, :rows, c] = r_ref[l, :, c]
            for i, (u, k, r) in enumerate(tiles):
                at = slice(rows + i * TILE, rows + (i + 1) * TILE)
                u0[l, at, c] = u
                kk[l, at, c] = k
                quad[l, at, c] = r

    place = place_ref[...]

    def done(c, values):
        for l, v in enumerate(values):
            new[l, :, c] = v[:rows]
        if c.stop % WIDE == 0:
            c = slice(c.stop - WIDE, c.stop)
            v = new[:, :, c].astype(jnp.bfloat16).reshape(levels * rows, WIDE)
            v = jnp.dot(place, v, preferred_element_type=jnp.float32).astype(jnp.bfloat16)
            at = 0
            for out in outs:
                out[:, c] = v[at : at + out.shape[0]]
                at += out.shape[0]

    if steps == 1:
        live = [(rows, rows + TILE, jnp.where(side, after, before) > 0)]
    else:
        live = [
            (rows, rows + TILE, jnp.where(row < TILE, after, 0) > 0),
            (rows + TILE, rows + 2 * TILE, jnp.where(row < TILE, before, 0) > 0),
        ]
    sections(steps, (levels, rows + steps * TILE, cells), fill, live, done, *scratch)


def advance(steps, state, kappa, rate, faces, place, parts):
    levels, rows, cells = state.shape
    slots = place.shape[0]
    out = [jax.ShapeDtypeStruct(state.shape, jnp.float32)] if steps > 1 else []
    out += [jax.ShapeDtypeStruct((slots // parts, cells), jnp.bfloat16)] * parts
    scratch = [] if steps > 1 else [pltpu.VMEM(state.shape, jnp.float32)]
    vmem = pl.BlockSpec(memory_space=pltpu.VMEM)
    return pl.pallas_call(
        functools.partial(steps_kernel, steps),
        out_shape=out,
        in_specs=[vmem] * (4 + len(faces)),
        out_specs=[vmem] * len(out),
        scratch_shapes=scratch
        + [pltpu.VMEM((levels, rows + steps * TILE, cells), jnp.float32)] * 10,
        compiler_params=pltpu.CompilerParams(vmem_limit_bytes=VMEM),
        cost_estimate=pl.CostEstimate(
            flops=120 * steps * levels * rows * cells,
            bytes_accessed=22 * levels * rows * cells,
            transcendentals=0,
        ),
    )(state, kappa, rate, *faces, place)


def vmem_call(kernel, args, out, **kw):
    vmem = pl.BlockSpec(memory_space=pltpu.VMEM)
    return pl.pallas_call(
        kernel,
        out_shape=out,
        in_specs=kw.pop("in_specs", [vmem] * len(args)),
        out_specs=kw.pop("out_specs", [vmem] * len(out)),
        compiler_params=pltpu.CompilerParams(vmem_limit_bytes=16 * 1024 * 1024),
        **kw,
    )(*args)


def weave_kernel(mine_ref, theirs_ref, *outs):
    odd = lax.axis_index("gx") % 2 == 1
    size = outs[0].shape[0] // 2
    for p, out in enumerate(outs):
        a, b = mine_ref[p * size : (p + 1) * size], theirs_ref[p * size : (p + 1) * size]
        out[:size] = jnp.where(odd, b, a)
        out[size:] = jnp.where(odd, a, b)


def put_kernel(part_ref, out_ref, sem):
    copy = pltpu.make_async_copy(part_ref, out_ref.at[0], sem)
    copy.start()
    copy.wait()


def put_blocks_kernel(which, *refs):
    blocks, out_ref, sems = refs[: len(which)], refs[-2], refs[-1]
    chip = lax.axis_index("gx") // 2
    copies = []
    for i, (p, ref) in enumerate(zip(which, blocks, strict=True)):
        size = ref.shape[0]
        at = pl.multiple_of((chip ^ p) * size, size)
        copies.append(
            pltpu.make_async_copy(ref, out_ref.at[1, pl.ds(at, size)], sems.at[i])
        )
    for copy in copies:
        copy.start()
    for copy in copies:
        copy.wait()


def placing(dest, block_of, writers, per_dev):
    slots = 2 * per_dev
    capacity = slots // writers
    onehot = (dest == jnp.arange(writers, dtype=jnp.int32)[None, :]).astype(jnp.float32)
    row_ids = jnp.arange(per_dev, dtype=jnp.int32)
    lower = (row_ids[:, None] > row_ids[None, :]).astype(jnp.float32)
    before = jnp.dot(lower, onehot, preferred_element_type=jnp.float32)
    ranks = jnp.sum(before * onehot, axis=1).astype(jnp.int32)
    target = block_of(dest[:, 0]) * capacity + ranks
    return (jnp.arange(slots, dtype=jnp.int32)[:, None] == target[None, :]).astype(jnp.bfloat16)


def shards(initial, kappa, rate, writer):
    n = lax.axis_size("gx")
    levels, rows, cells = initial.shape
    per_dev = levels * rows
    slots = 2 * per_dev
    capacity = slots // n
    by_core = [(i, i ^ 1) for i in range(n)]
    by_chip = [(i, i + 1) for i in range(1, n - 1, 2)] + [(i + 1, i) for i in range(1, n - 1, 2)]

    def route(packed):
        return lax.all_to_all(packed, "gx", split_axis=0, concat_axis=0, tiled=True)

    to_core, to_chip, deep = pack_faces(initial, kappa, rate)
    faces = [lax.ppermute(to_core, "gx", by_core), lax.ppermute(to_chip, "gx", by_chip)]
    deep = lax.ppermute(deep, "gx", by_chip)
    place = placing(writer[0], lambda d: d, n, per_dev)
    (packed,) = advance(1, initial, kappa, rate, faces, place, 1)
    packed, deep = lax.optimization_barrier((packed, deep))
    first = route(packed)
    faces = faces + [deep]
    if capacity % 16 or n & (n - 1):
        place = placing(writer[1], lambda d: d, n, per_dev)
        state, packed = advance(2, initial, kappa, rate, faces, place, 1)
        return state, jnp.stack([first, route(packed)])

    chips = n // 2
    me = lax.axis_index("gx")
    place = placing(writer[1], lambda d: ((d ^ me) & 1) * chips + ((d ^ me) >> 1), n, per_dev)
    state, mine, theirs = advance(2, initial, kappa, rate, faces, place, 2)
    theirs = lax.ppermute(theirs, "gx", by_core)
    block = jax.ShapeDtypeStruct((2 * capacity, cells), jnp.bfloat16)
    frames = jax.ShapeDtypeStruct((STEPS, slots, cells), jnp.bfloat16)
    hbm = pl.BlockSpec(memory_space=pltpu.HBM)
    vmem = pl.BlockSpec(memory_space=pltpu.VMEM)
    blocks = vmem_call(weave_kernel, (mine, theirs), [block] * chips)
    got = [blocks[0]]
    for p in range(1, chips):
        got.append(lax.ppermute(blocks[p], "gx", [(i, i ^ (2 * p)) for i in range(n)]))
    (out,) = vmem_call(
        put_kernel,
        (first,),
        [frames],
        out_specs=[hbm],
        scratch_shapes=[pltpu.SemaphoreType.DMA],
    )
    (out,) = vmem_call(
        functools.partial(put_blocks_kernel, range(chips)),
        (*got, out),
        [frames],
        in_specs=[vmem] * chips + [hbm],
        out_specs=[hbm],
        scratch_shapes=[pltpu.SemaphoreType.DMA((chips,))],
        input_output_aliases={chips: 0},
    )
    return state, out


def solution(mesh):
    spec = P("runs", "gx", None)
    return jax.shard_map(
        shards, mesh=mesh, in_specs=(spec,) * 4, out_specs=(spec, spec), check_vma=False
    )
```

```python
import functools

import jax
import jax.numpy as jnp
from jax import lax
from jax.experimental import pallas as pl
from jax.experimental.pallas import tpu as pltpu
from jax.sharding import PartitionSpec as P

STEPS = 2
DT = 0.15
LANES = 128
TILE = 8
WIDE = 2 * LANES
VMEM = 30 * 1024 * 1024


def roll_rows(v, shift):
    shift = shift % v.shape[0]
    return pltpu.roll(v, shift, 0) if shift else v


def pack_kernel(u_ref, k_ref, r_ref, core_ref, chip_ref, deep_ref, top, bot, sems):
    levels, rows, cells = u_ref.shape
    copies = []
    for i, ref in enumerate((u_ref, k_ref, r_ref)):
        copies.append(pltpu.make_async_copy(ref.at[:, :TILE], top.at[i], sems.at[0, i]))
        copies.append(pltpu.make_async_copy(ref.at[:, rows - TILE :], bot.at[i], sems.at[1, i]))
    for copy in copies:
        copy.start()
    for copy in copies:
        copy.wait()
    even = lax.axis_index("gx") % 2 == 0
    row = lax.broadcasted_iota(jnp.int32, (TILE, LANES), 0)
    near = levels * TILE
    for j in range(0, cells, LANES):
        c = slice(j, j + LANES)
        first, last, deep_first, deep_last = [], [], [], []
        end_first = end_last = zero = jnp.zeros((TILE, LANES), jnp.float32)
        for l in range(levels):
            u, k, r = top[0, l, :, c], top[1, l, :, c], top[2, l, :, c]
            k5 = roll_rows(k, 5)
            first.append(jnp.where(row < 3, u, jnp.where(row < 5, roll_rows(r, 3), k5)))
            v = jnp.where(row < 3, k5, roll_rows(r, 4))
            deep_first.append(jnp.where((row < 3) | (row >= 6), v, u))
            end_first = jnp.where(row == l, roll_rows(r, l - 4), end_first)
            u, k, r = bot[0, l, :, c], bot[1, l, :, c], bot[2, l, :, c]
            k3 = roll_rows(k, 3)
            last.append(jnp.where(row < 5, jnp.where(row < 3, k3, roll_rows(r, 5)), u))
            v = jnp.where(row < 2, roll_rows(r, 4), k3)
            deep_last.append(jnp.where((row < 2) | (row >= 5), v, u))
            end_last = jnp.where(row == l, roll_rows(r, l - 3), end_last)
        a = jnp.concatenate(first + deep_first + [end_first, zero], 0)
        b = jnp.concatenate(last + deep_last + [end_last, zero], 0)
        core_ref[:, c] = jnp.where(even, b, a).astype(jnp.bfloat16)
        chip = jnp.where(even, a, b).astype(jnp.bfloat16)
        chip_ref[:, c] = chip[:near]
        deep_ref[:, c] = chip[near : near + deep_ref.shape[0]]


def pack_faces(u, k, r):
    levels, _, cells = u.shape
    hbm = pl.BlockSpec(memory_space=pltpu.HBM)
    sizes = [(2 * levels + 2) * TILE, levels * TILE, (levels + 2) * TILE]
    return pl.pallas_call(
        pack_kernel,
        out_shape=[jax.ShapeDtypeStruct((size, cells), jnp.bfloat16) for size in sizes],
        in_specs=[hbm] * 3,
        out_specs=[pl.BlockSpec(memory_space=pltpu.VMEM)] * 3,
        scratch_shapes=[pltpu.VMEM((3, levels, TILE, cells), jnp.float32)] * 2
        + [pltpu.SemaphoreType.DMA((2, 3))],
        compiler_params=pltpu.CompilerParams(vmem_limit_bytes=60 * 1024 * 1024),
    )(u, k, r)


def sections(steps, shape, fill, live, done, u0, u1, u2, xp, xm, yp, ym, zp, lin, quad):
    levels, ext, cells = shape
    chunks = cells // LANES
    lane = lax.broadcasted_iota(jnp.int32, (ext, LANES), 1)

    def cols(j):
        j = j % chunks
        return slice(j * LANES, (j + 1) * LANES)

    kk = u2

    def left_right(src, l):
        right, left, here = {}, {}, {}

        def rots(j):
            j = j % chunks
            if j not in here:
                v = src[l, :, cols(j)]
                here[j] = v
                right[j] = pltpu.roll(v, LANES - 1, 1)
                left[j] = pltpu.roll(v, 1, 1)
            return j

        def at(j):
            a, b, d = rots(j - 1), rots(j), rots(j + 1)
            return (
                here[b],
                jnp.where(lane == LANES - 1, right[d], right[b]),
                jnp.where(lane == 0, left[a], left[b]),
            )

        return at

    half = 0.5 * DT
    ats = [left_right(kk, l) for l in range(levels)]
    for j in range(chunks):
        fill(j, u0, kk, quad)
    for j in range(chunks):
        c = cols(j)
        for l in range(levels):
            k, k_right, k_left = ats[l](j)
            a = half * (k + pltpu.roll(k, ext - 1, 0))
            b = pltpu.roll(a, 1, 0)
            d, e = half * (k + k_right), half * (k + k_left)
            xp[l, :, c], xm[l, :, c], yp[l, :, c], ym[l, :, c] = a, b, d, e
            total = a + b + d + e
            if l < levels - 1:
                f = half * (k + kk[l + 1, :, c])
                zp[l, :, c] = f
                total = total + f
            if l > 0:
                total = total + zp[l - 1, :, c]
            lin[l, :, c] = 1.0 + quad[l, :, c] - total

    def euler(src, ats, l, j):
        c = cols(j)
        u, u_right, u_left = ats[l](j)
        out = u * (lin[l, :, c] - quad[l, :, c] * u)
        out = out + xp[l, :, c] * pltpu.roll(u, ext - 1, 0) + xm[l, :, c] * pltpu.roll(u, 1, 0)
        out = out + yp[l, :, c] * u_right + ym[l, :, c] * u_left
        if l < levels - 1:
            out = out + zp[l, :, c] * src[l + 1, :, c]
        if l > 0:
            out = out + zp[l - 1, :, c] * src[l - 1, :, c]
        return out

    def masked(dst, l, c, v):
        at = 0
        for start, stop, keep in live:
            if at < start:
                dst[l, at:start, c] = v[at:start]
            dst[l, start:stop, c] = jnp.where(keep, v[start:stop], 0.0)
            at = stop
        if at < ext:
            dst[l, at:, c] = v[at:]

    for step in range(steps):
        ats = [left_right(u0, l) for l in range(levels)]
        for j in range(chunks):
            for l in range(levels):
                masked(u1, l, cols(j), euler(u0, ats, l, j))
        ats = [left_right(u1, l) for l in range(levels)]
        for j in range(chunks):
            for l in range(levels):
                c = cols(j)
                masked(u2, l, c, 0.75 * u0[l, :, c] + 0.25 * euler(u1, ats, l, j))
        ats = [left_right(u2, l) for l in range(levels)]
        for j in range(chunks):
            c = cols(j)
            values = [
                (1.0 / 3.0) * u0[l, :, c] + (2.0 / 3.0) * euler(u2, ats, l, j)
                for l in range(levels)
            ]
            if step == steps - 1:
                done(c, values)
            else:
                for l in range(levels):
                    masked(u0, l, c, values[l])


def grid_ends():
    me, n = lax.axis_index("gx"), lax.axis_size("gx")
    return (me < n - 1).astype(jnp.int32), (me > 0).astype(jnp.int32), me % 2 == 0


def sides(core, chip, even):
    core, chip = core.astype(jnp.float32), chip.astype(jnp.float32)
    return jnp.where(even, core, chip), jnp.where(even, chip, core)


def steps_kernel(steps, u_ref, k_ref, r_ref, core_ref, chip_ref, *refs):
    scratch, refs = refs[-10:], refs[:-10]
    if steps == 1:
        place_ref, *outs, new = refs
    else:
        deep_ref, place_ref, new, *outs = refs
    levels, rows, cells = u_ref.shape
    near = levels * TILE
    after, before, even = grid_ends()
    row = lax.broadcasted_iota(jnp.int32, (TILE, LANES), 0)
    side = row < TILE // 2

    def faces(c):
        below, above = sides(core_ref[:near, c], chip_ref[:, c], even)
        tiles = [slice(l * TILE, (l + 1) * TILE) for l in range(levels)]
        if steps == 1:
            for t in tiles:
                b, a = below[t], above[t]
                yield [
                    (
                        jnp.where(side, b, a),
                        jnp.where(side, roll_rows(b, 3), roll_rows(a, 5)),
                        jnp.where(side, roll_rows(b, 5), roll_rows(a, 3)),
                    )
                ]
            return
        below2, above2 = sides(core_ref[near:, c], deep_ref[:, c], even)
        r_below, r_above = below2[near : near + TILE], above2[near : near + TILE]
        for l, t in enumerate(tiles):
            b, a, b2, a2 = below[t], above[t], below2[t], above2[t]
            rb = jnp.where(row < 4, roll_rows(b2, 4), roll_rows(r_below, 4 - l))
            ra = jnp.where(row >= 4, roll_rows(a2, 4), roll_rows(r_above, 3 - l))
            b_tiles = (
                jnp.where(row < 3, b, b2),
                roll_rows(jnp.where(row >= 5, b, b2), 3),
                jnp.where(row < 2, roll_rows(b, 5), rb),
            )
            a_tiles = (
                jnp.where(row >= 5, a, a2),
                roll_rows(jnp.where(row < 3, a, a2), 5),
                jnp.where(row >= 6, roll_rows(a, 3), ra),
            )
            yield [
                [jnp.where(row < 6, v, 0.0) for v in b_tiles],
                [jnp.where(row >= 2, v, 0.0) for v in a_tiles],
            ]

    def fill(j, u0, kk, quad):
        c = slice(j * LANES, (j + 1) * LANES)
        for l, tiles in enumerate(faces(c)):
            u0[l, :rows, c] = u_ref[l, :, c]
            kk[l, :rows, c] = k_ref[l, :, c]
            quad[l, :rows, c] = DT * r_ref[l, :, c]
            for i, (u, k, r) in enumerate(tiles):
                at = slice(rows + i * TILE, rows + (i + 1) * TILE)
                u0[l, at, c] = u
                kk[l, at, c] = k
                quad[l, at, c] = DT * r

    place = place_ref[...]

    def done(c, values):
        for l, v in enumerate(values):
            new[l, :, c] = v[:rows]
        if c.stop % WIDE == 0:
            c = slice(c.stop - WIDE, c.stop)
            v = new[:, :, c].astype(jnp.bfloat16).reshape(levels * rows, WIDE)
            v = jnp.dot(place, v, preferred_element_type=jnp.float32).astype(jnp.bfloat16)
            at = 0
            for out in outs:
                out[:, c] = v[at : at + out.shape[0]]
                at += out.shape[0]

    if steps == 1:
        live = [(rows, rows + TILE, jnp.where(side, after, before) > 0)]
    else:
        live = [
            (rows, rows + TILE, jnp.where(row < TILE, after, 0) > 0),
            (rows + TILE, rows + 2 * TILE, jnp.where(row < TILE, before, 0) > 0),
        ]
    sections(steps, (levels, rows + steps * TILE, cells), fill, live, done, *scratch)


def advance(steps, state, kappa, rate, faces, place, parts):
    levels, rows, cells = state.shape
    slots = place.shape[0]
    out = [jax.ShapeDtypeStruct(state.shape, jnp.float32)] if steps > 1 else []
    out += [jax.ShapeDtypeStruct((slots // parts, cells), jnp.bfloat16)] * parts
    scratch = [] if steps > 1 else [pltpu.VMEM(state.shape, jnp.float32)]
    vmem = pl.BlockSpec(memory_space=pltpu.VMEM)
    return pl.pallas_call(
        functools.partial(steps_kernel, steps),
        out_shape=out,
        in_specs=[vmem] * (4 + len(faces)),
        out_specs=[vmem] * len(out),
        scratch_shapes=scratch
        + [pltpu.VMEM((levels, rows + steps * TILE, cells), jnp.float32)] * 10,
        compiler_params=pltpu.CompilerParams(vmem_limit_bytes=VMEM),
        cost_estimate=pl.CostEstimate(
            flops=120 * steps * levels * rows * cells,
            bytes_accessed=22 * levels * rows * cells,
            transcendentals=0,
        ),
    )(state, kappa, rate, *faces, place)


def vmem_call(kernel, args, out, **kw):
    vmem = pl.BlockSpec(memory_space=pltpu.VMEM)
    return pl.pallas_call(
        kernel,
        out_shape=out,
        in_specs=kw.pop("in_specs", [vmem] * len(args)),
        out_specs=kw.pop("out_specs", [vmem] * len(out)),
        compiler_params=pltpu.CompilerParams(vmem_limit_bytes=16 * 1024 * 1024),
        **kw,
    )(*args)


def weave_kernel(mine_ref, theirs_ref, *outs):
    odd = lax.axis_index("gx") % 2 == 1
    size = outs[0].shape[0] // 2
    for p, out in enumerate(outs):
        a, b = mine_ref[p * size : (p + 1) * size], theirs_ref[p * size : (p + 1) * size]
        out[:size] = jnp.where(odd, b, a)
        out[size:] = jnp.where(odd, a, b)


def put_kernel(part_ref, out_ref, sem):
    copy = pltpu.make_async_copy(part_ref, out_ref.at[0], sem)
    copy.start()
    copy.wait()


def put_blocks_kernel(which, *refs):
    blocks, out_ref, sems = refs[: len(which)], refs[-2], refs[-1]
    chip = lax.axis_index("gx") // 2
    copies = []
    for i, (p, ref) in enumerate(zip(which, blocks, strict=True)):
        size = ref.shape[0]
        at = pl.multiple_of((chip ^ p) * size, size)
        copies.append(
            pltpu.make_async_copy(ref, out_ref.at[1, pl.ds(at, size)], sems.at[i])
        )
    for copy in copies:
        copy.start()
    for copy in copies:
        copy.wait()


def placing(dest, block_of, writers, per_dev):
    slots = 2 * per_dev
    capacity = slots // writers
    onehot = (dest == jnp.arange(writers, dtype=jnp.int32)[None, :]).astype(jnp.float32)
    row_ids = jnp.arange(per_dev, dtype=jnp.int32)
    lower = (row_ids[:, None] > row_ids[None, :]).astype(jnp.float32)
    before = jnp.dot(lower, onehot, preferred_element_type=jnp.float32)
    ranks = jnp.sum(before * onehot, axis=1).astype(jnp.int32)
    target = block_of(dest[:, 0]) * capacity + ranks
    return (jnp.arange(slots, dtype=jnp.int32)[:, None] == target[None, :]).astype(jnp.bfloat16)


def shards(initial, kappa, rate, writer):
    n = lax.axis_size("gx")
    levels, rows, cells = initial.shape
    per_dev = levels * rows
    slots = 2 * per_dev
    capacity = slots // n
    by_core = [(i, i ^ 1) for i in range(n)]
    by_chip = [(i, i + 1) for i in range(1, n - 1, 2)] + [(i + 1, i) for i in range(1, n - 1, 2)]

    def route(packed):
        return lax.all_to_all(packed, "gx", split_axis=0, concat_axis=0, tiled=True)

    to_core, to_chip, deep = pack_faces(initial, kappa, rate)
    faces = [lax.ppermute(to_core, "gx", by_core), lax.ppermute(to_chip, "gx", by_chip)]
    deep = lax.ppermute(deep, "gx", by_chip)
    place = placing(writer[0], lambda d: d, n, per_dev)
    (packed,) = advance(1, initial, kappa, rate, faces, place, 1)
    packed, deep = lax.optimization_barrier((packed, deep))
    first = route(packed)
    faces = faces + [deep]
    if capacity % 16 or n & (n - 1):
        place = placing(writer[1], lambda d: d, n, per_dev)
        state, packed = advance(2, initial, kappa, rate, faces, place, 1)
        return state, jnp.stack([first, route(packed)])

    chips = n // 2
    me = lax.axis_index("gx")
    place = placing(writer[1], lambda d: ((d ^ me) & 1) * chips + ((d ^ me) >> 1), n, per_dev)
    state, mine, theirs = advance(2, initial, kappa, rate, faces, place, 2)
    theirs = lax.ppermute(theirs, "gx", by_core)
    block = jax.ShapeDtypeStruct((2 * capacity, cells), jnp.bfloat16)
    frames = jax.ShapeDtypeStruct((STEPS, slots, cells), jnp.bfloat16)
    hbm = pl.BlockSpec(memory_space=pltpu.HBM)
    vmem = pl.BlockSpec(memory_space=pltpu.VMEM)
    blocks = vmem_call(weave_kernel, (mine, theirs), [block] * chips)
    got = [blocks[0]]
    for p in range(1, chips):
        got.append(lax.ppermute(blocks[p], "gx", [(i, i ^ (2 * p)) for i in range(n)]))
    (out,) = vmem_call(
        put_kernel,
        (first,),
        [frames],
        out_specs=[hbm],
        scratch_shapes=[pltpu.SemaphoreType.DMA],
    )
    for which in (range(chips - 2), range(chips - 2, chips)):
        (out,) = vmem_call(
            functools.partial(put_blocks_kernel, which),
            (*[got[p] for p in which], out),
            [frames],
            in_specs=[vmem] * len(which) + [hbm],
            out_specs=[hbm],
            scratch_shapes=[pltpu.SemaphoreType.DMA((chips,))],
            input_output_aliases={len(which): 0},
        )
    return state, out


def solution(mesh):
    spec = P("runs", "gx", None)
    return jax.shard_map(
        shards, mesh=mesh, in_specs=(spec,) * 4, out_specs=(spec, spec), check_vma=False
    )
```

```python
import functools

import jax
import jax.numpy as jnp
from jax import lax
from jax.experimental import pallas as pl
from jax.experimental.pallas import tpu as pltpu
from jax.sharding import PartitionSpec as P

STEPS = 2
DT = 0.15
LANES = 128
TILE = 8
WIDE = 2 * LANES
VMEM = 30 * 1024 * 1024


def roll_rows(v, shift):
    shift = shift % v.shape[0]
    return pltpu.roll(v, shift, 0) if shift else v


def pack_kernel(u_ref, k_ref, r_ref, core_ref, chip_ref, deep_ref, top, bot, sems):
    levels, rows, cells = u_ref.shape
    copies = []
    for i, ref in enumerate((u_ref, k_ref, r_ref)):
        copies.append(pltpu.make_async_copy(ref.at[:, :TILE], top.at[i], sems.at[0, i]))
        copies.append(pltpu.make_async_copy(ref.at[:, rows - TILE :], bot.at[i], sems.at[1, i]))
    for copy in copies:
        copy.start()
    for copy in copies:
        copy.wait()
    even = lax.axis_index("gx") % 2 == 0
    row = lax.broadcasted_iota(jnp.int32, (TILE, LANES), 0)
    near = levels * TILE
    for j in range(0, cells, LANES):
        c = slice(j, j + LANES)
        first, last, deep_first, deep_last = [], [], [], []
        end_first = end_last = zero = jnp.zeros((TILE, LANES), jnp.float32)
        for l in range(levels):
            u, k, r = top[0, l, :, c], top[1, l, :, c], top[2, l, :, c]
            k5 = roll_rows(k, 5)
            first.append(jnp.where(row < 3, u, jnp.where(row < 5, roll_rows(r, 3), k5)))
            v = jnp.where(row < 3, k5, roll_rows(r, 4))
            deep_first.append(jnp.where((row < 3) | (row >= 6), v, u))
            end_first = jnp.where(row == l, roll_rows(r, l - 4), end_first)
            u, k, r = bot[0, l, :, c], bot[1, l, :, c], bot[2, l, :, c]
            k3 = roll_rows(k, 3)
            last.append(jnp.where(row < 5, jnp.where(row < 3, k3, roll_rows(r, 5)), u))
            v = jnp.where(row < 2, roll_rows(r, 4), k3)
            deep_last.append(jnp.where((row < 2) | (row >= 5), v, u))
            end_last = jnp.where(row == l, roll_rows(r, l - 3), end_last)
        a = jnp.concatenate(first + deep_first + [end_first, zero], 0)
        b = jnp.concatenate(last + deep_last + [end_last, zero], 0)
        core_ref[:, c] = jnp.where(even, b, a).astype(jnp.bfloat16)
        chip = jnp.where(even, a, b).astype(jnp.bfloat16)
        chip_ref[:, c] = chip[:near]
        deep_ref[:, c] = chip[near : near + deep_ref.shape[0]]


def pack_faces(u, k, r):
    levels, _, cells = u.shape
    hbm = pl.BlockSpec(memory_space=pltpu.HBM)
    sizes = [(2 * levels + 2) * TILE, levels * TILE, (levels + 1) * TILE]
    return pl.pallas_call(
        pack_kernel,
        out_shape=[jax.ShapeDtypeStruct((size, cells), jnp.bfloat16) for size in sizes],
        in_specs=[hbm] * 3,
        out_specs=[pl.BlockSpec(memory_space=pltpu.VMEM)] * 3,
        scratch_shapes=[pltpu.VMEM((3, levels, TILE, cells), jnp.float32)] * 2
        + [pltpu.SemaphoreType.DMA((2, 3))],
        compiler_params=pltpu.CompilerParams(vmem_limit_bytes=60 * 1024 * 1024),
    )(u, k, r)


def sections(steps, shape, fill, live, done, u0, u1, u2, xp, xm, yp, ym, zp, lin, quad):
    levels, ext, cells = shape
    chunks = cells // LANES
    lane = lax.broadcasted_iota(jnp.int32, (ext, LANES), 1)

    def cols(j):
        j = j % chunks
        return slice(j * LANES, (j + 1) * LANES)

    kk = u2

    def left_right(src, l):
        right, left, here = {}, {}, {}

        def rots(j):
            j = j % chunks
            if j not in here:
                v = src[l, :, cols(j)]
                here[j] = v
                right[j] = pltpu.roll(v, LANES - 1, 1)
                left[j] = pltpu.roll(v, 1, 1)
            return j

        def at(j):
            a, b, d = rots(j - 1), rots(j), rots(j + 1)
            return (
                here[b],
                jnp.where(lane == LANES - 1, right[d], right[b]),
                jnp.where(lane == 0, left[a], left[b]),
            )

        return at

    half = 0.5 * DT
    ats = [left_right(kk, l) for l in range(levels)]
    for j in range(chunks):
        fill(j, u0, kk, quad)
    for j in range(chunks):
        c = cols(j)
        for l in range(levels):
            k, k_right, k_left = ats[l](j)
            a = half * (k + pltpu.roll(k, ext - 1, 0))
            b = pltpu.roll(a, 1, 0)
            d, e = half * (k + k_right), half * (k + k_left)
            xp[l, :, c], xm[l, :, c], yp[l, :, c], ym[l, :, c] = a, b, d, e
            total = a + b + d + e
            if l < levels - 1:
                f = half * (k + kk[l + 1, :, c])
                zp[l, :, c] = f
                total = total + f
            if l > 0:
                total = total + zp[l - 1, :, c]
            lin[l, :, c] = 1.0 + quad[l, :, c] - total

    def euler(src, ats, l, j):
        c = cols(j)
        u, u_right, u_left = ats[l](j)
        out = u * (lin[l, :, c] - quad[l, :, c] * u)
        out = out + xp[l, :, c] * pltpu.roll(u, ext - 1, 0) + xm[l, :, c] * pltpu.roll(u, 1, 0)
        out = out + yp[l, :, c] * u_right + ym[l, :, c] * u_left
        if l < levels - 1:
            out = out + zp[l, :, c] * src[l + 1, :, c]
        if l > 0:
            out = out + zp[l - 1, :, c] * src[l - 1, :, c]
        return out

    def masked(dst, l, c, v):
        at = 0
        for start, stop, keep in live:
            if at < start:
                dst[l, at:start, c] = v[at:start]
            dst[l, start:stop, c] = jnp.where(keep, v[start:stop], 0.0)
            at = stop
        if at < ext:
            dst[l, at:, c] = v[at:]

    for step in range(steps):
        ats = [left_right(u0, l) for l in range(levels)]
        for j in range(chunks):
            for l in range(levels):
                masked(u1, l, cols(j), euler(u0, ats, l, j))
        ats = [left_right(u1, l) for l in range(levels)]
        for j in range(chunks):
            for l in range(levels):
                c = cols(j)
                masked(u2, l, c, 0.75 * u0[l, :, c] + 0.25 * euler(u1, ats, l, j))
        ats = [left_right(u2, l) for l in range(levels)]
        for j in range(chunks):
            c = cols(j)
            values = [
                (1.0 / 3.0) * u0[l, :, c] + (2.0 / 3.0) * euler(u2, ats, l, j)
                for l in range(levels)
            ]
            if step == steps - 1:
                done(c, values)
            else:
                for l in range(levels):
                    masked(u0, l, c, values[l])


def grid_ends():
    me, n = lax.axis_index("gx"), lax.axis_size("gx")
    return (me < n - 1).astype(jnp.int32), (me > 0).astype(jnp.int32), me % 2 == 0


def sides(core, chip, even):
    core, chip = core.astype(jnp.float32)[: chip.shape[0]], chip.astype(jnp.float32)
    return jnp.where(even, core, chip), jnp.where(even, chip, core)


def steps_kernel(steps, u_ref, k_ref, r_ref, core_ref, chip_ref, *refs):
    scratch, refs = refs[-10:], refs[:-10]
    if steps == 1:
        place_ref, *outs, new = refs
    else:
        deep_ref, place_ref, new, *outs = refs
    levels, rows, cells = u_ref.shape
    near = levels * TILE
    after, before, even = grid_ends()
    row = lax.broadcasted_iota(jnp.int32, (TILE, LANES), 0)
    side = row < TILE // 2

    def faces(c):
        below, above = sides(core_ref[:near, c], chip_ref[:, c], even)
        tiles = [slice(l * TILE, (l + 1) * TILE) for l in range(levels)]
        if steps == 1:
            for t in tiles:
                b, a = below[t], above[t]
                yield [
                    (
                        jnp.where(side, b, a),
                        jnp.where(side, roll_rows(b, 3), roll_rows(a, 5)),
                        jnp.where(side, roll_rows(b, 5), roll_rows(a, 3)),
                    )
                ]
            return
        below2, above2 = sides(core_ref[near:, c], deep_ref[:, c], even)
        r_below, r_above = below2[near : near + TILE], above2[near : near + TILE]
        for l, t in enumerate(tiles):
            b, a, b2, a2 = below[t], above[t], below2[t], above2[t]
            rb = jnp.where(row < 4, roll_rows(b2, 4), roll_rows(r_below, 4 - l))
            ra = jnp.where(row >= 4, roll_rows(a2, 4), roll_rows(r_above, 3 - l))
            b_tiles = (
                jnp.where(row < 3, b, b2),
                roll_rows(jnp.where(row >= 5, b, b2), 3),
                jnp.where(row < 2, roll_rows(b, 5), rb),
            )
            a_tiles = (
                jnp.where(row >= 5, a, a2),
                roll_rows(jnp.where(row < 3, a, a2), 5),
                jnp.where(row >= 6, roll_rows(a, 3), ra),
            )
            yield [
                [jnp.where(row < 6, v, 0.0) for v in b_tiles],
                [jnp.where(row >= 2, v, 0.0) for v in a_tiles],
            ]

    def fill(j, u0, kk, quad):
        c = slice(j * LANES, (j + 1) * LANES)
        for l, tiles in enumerate(faces(c)):
            u0[l, :rows, c] = u_ref[l, :, c]
            kk[l, :rows, c] = k_ref[l, :, c]
            quad[l, :rows, c] = DT * r_ref[l, :, c]
            for i, (u, k, r) in enumerate(tiles):
                at = slice(rows + i * TILE, rows + (i + 1) * TILE)
                u0[l, at, c] = u
                kk[l, at, c] = k
                quad[l, at, c] = DT * r

    place = place_ref[...]

    def done(c, values):
        for l, v in enumerate(values):
            new[l, :, c] = v[:rows]
        if c.stop % WIDE == 0:
            c = slice(c.stop - WIDE, c.stop)
            v = new[:, :, c].astype(jnp.bfloat16).reshape(levels * rows, WIDE)
            v = jnp.dot(place, v, preferred_element_type=jnp.float32).astype(jnp.bfloat16)
            at = 0
            for out in outs:
                out[:, c] = v[at : at + out.shape[0]]
                at += out.shape[0]

    if steps == 1:
        live = [(rows, rows + TILE, jnp.where(side, after, before) > 0)]
    else:
        live = [
            (rows, rows + TILE, jnp.where(row < TILE, after, 0) > 0),
            (rows + TILE, rows + 2 * TILE, jnp.where(row < TILE, before, 0) > 0),
        ]
    sections(steps, (levels, rows + steps * TILE, cells), fill, live, done, *scratch)


def advance(steps, state, kappa, rate, faces, place, parts):
    levels, rows, cells = state.shape
    slots = place.shape[0]
    out = [jax.ShapeDtypeStruct(state.shape, jnp.float32)] if steps > 1 else []
    out += [jax.ShapeDtypeStruct((slots // parts, cells), jnp.bfloat16)] * parts
    scratch = [] if steps > 1 else [pltpu.VMEM(state.shape, jnp.float32)]
    vmem = pl.BlockSpec(memory_space=pltpu.VMEM)
    return pl.pallas_call(
        functools.partial(steps_kernel, steps),
        out_shape=out,
        in_specs=[vmem] * (4 + len(faces)),
        out_specs=[vmem] * len(out),
        scratch_shapes=scratch
        + [pltpu.VMEM((levels, rows + steps * TILE, cells), jnp.float32)] * 10,
        compiler_params=pltpu.CompilerParams(vmem_limit_bytes=VMEM),
        cost_estimate=pl.CostEstimate(
            flops=120 * steps * levels * rows * cells,
            bytes_accessed=22 * levels * rows * cells,
            transcendentals=0,
        ),
    )(state, kappa, rate, *faces, place)


def vmem_call(kernel, args, out, **kw):
    vmem = pl.BlockSpec(memory_space=pltpu.VMEM)
    return pl.pallas_call(
        kernel,
        out_shape=out,
        in_specs=kw.pop("in_specs", [vmem] * len(args)),
        out_specs=kw.pop("out_specs", [vmem] * len(out)),
        compiler_params=pltpu.CompilerParams(vmem_limit_bytes=16 * 1024 * 1024),
        **kw,
    )(*args)


def weave_kernel(mine_ref, theirs_ref, *outs):
    odd = lax.axis_index("gx") % 2 == 1
    size = outs[0].shape[0] // 2
    for p, out in enumerate(outs):
        a, b = mine_ref[p * size : (p + 1) * size], theirs_ref[p * size : (p + 1) * size]
        out[:size] = jnp.where(odd, b, a)
        out[size:] = jnp.where(odd, a, b)


def put_kernel(part_ref, out_ref, sem):
    copy = pltpu.make_async_copy(part_ref, out_ref.at[0], sem)
    copy.start()
    copy.wait()


def put_blocks_kernel(which, *refs):
    blocks, out_ref, sems = refs[: len(which)], refs[-2], refs[-1]
    chip = lax.axis_index("gx") // 2
    copies = []
    for i, (p, ref) in enumerate(zip(which, blocks, strict=True)):
        size = ref.shape[0]
        at = pl.multiple_of((chip ^ p) * size, size)
        copies.append(
            pltpu.make_async_copy(ref, out_ref.at[1, pl.ds(at, size)], sems.at[i])
        )
    for copy in copies:
        copy.start()
    for copy in copies:
        copy.wait()


def placing(dest, block_of, writers, per_dev):
    slots = 2 * per_dev
    capacity = slots // writers
    onehot = (dest == jnp.arange(writers, dtype=jnp.int32)[None, :]).astype(jnp.float32)
    row_ids = jnp.arange(per_dev, dtype=jnp.int32)
    lower = (row_ids[:, None] > row_ids[None, :]).astype(jnp.float32)
    before = jnp.dot(lower, onehot, preferred_element_type=jnp.float32)
    ranks = jnp.sum(before * onehot, axis=1).astype(jnp.int32)
    target = block_of(dest[:, 0]) * capacity + ranks
    return (jnp.arange(slots, dtype=jnp.int32)[:, None] == target[None, :]).astype(jnp.bfloat16)


def shards(initial, kappa, rate, writer):
    n = lax.axis_size("gx")
    levels, rows, cells = initial.shape
    per_dev = levels * rows
    slots = 2 * per_dev
    capacity = slots // n
    by_core = [(i, i ^ 1) for i in range(n)]
    by_chip = [(i, i + 1) for i in range(1, n - 1, 2)] + [(i + 1, i) for i in range(1, n - 1, 2)]

    def route(packed):
        return lax.all_to_all(packed, "gx", split_axis=0, concat_axis=0, tiled=True)

    to_core, to_chip, deep = pack_faces(initial, kappa, rate)
    faces = [lax.ppermute(to_core, "gx", by_core), lax.ppermute(to_chip, "gx", by_chip)]
    deep = lax.ppermute(deep, "gx", by_chip)
    place = placing(writer[0], lambda d: d, n, per_dev)
    (packed,) = advance(1, initial, kappa, rate, faces, place, 1)
    packed, deep = lax.optimization_barrier((packed, deep))
    first = route(packed)
    faces = faces + [deep]
    if capacity % 16 or n & (n - 1):
        place = placing(writer[1], lambda d: d, n, per_dev)
        state, packed = advance(2, initial, kappa, rate, faces, place, 1)
        return state, jnp.stack([first, route(packed)])

    chips = n // 2
    me = lax.axis_index("gx")
    place = placing(writer[1], lambda d: ((d ^ me) & 1) * chips + ((d ^ me) >> 1), n, per_dev)
    state, mine, theirs = advance(2, initial, kappa, rate, faces, place, 2)
    theirs = lax.ppermute(theirs, "gx", by_core)
    block = jax.ShapeDtypeStruct((2 * capacity, cells), jnp.bfloat16)
    frames = jax.ShapeDtypeStruct((STEPS, slots, cells), jnp.bfloat16)
    hbm = pl.BlockSpec(memory_space=pltpu.HBM)
    vmem = pl.BlockSpec(memory_space=pltpu.VMEM)
    blocks = vmem_call(weave_kernel, (mine, theirs), [block] * chips)
    got = [blocks[0]]
    for p in range(1, chips):
        got.append(lax.ppermute(blocks[p], "gx", [(i, i ^ (2 * p)) for i in range(n)]))
    (out,) = vmem_call(
        put_kernel,
        (first,),
        [frames],
        out_specs=[hbm],
        scratch_shapes=[pltpu.SemaphoreType.DMA],
    )
    for which in (range(chips - 2), range(chips - 2, chips)):
        (out,) = vmem_call(
            functools.partial(put_blocks_kernel, which),
            (*[got[p] for p in which], out),
            [frames],
            in_specs=[vmem] * len(which) + [hbm],
            out_specs=[hbm],
            scratch_shapes=[pltpu.SemaphoreType.DMA((chips,))],
            input_output_aliases={len(which): 0},
        )
    return state, out


def solution(mesh):
    spec = P("runs", "gx", None)
    return jax.shard_map(
        shards, mesh=mesh, in_specs=(spec,) * 4, out_specs=(spec, spec), check_vma=False
    )
```
